32 devices in a mesh: context: 4 (over z), mirror: 2 (over core), tensor: 4 (over y, x).
Axes of the slice: x: 2, y: 2, z: 4, core: 2. Of those that a mesh axis runs over, the one named last changes fastest.
Arguments:
- hyena_q: bfloat16 [1024, 8192], P(('context', 'mirror'), 'tensor'), may hold values from -57 to 57
- hyena_k: bfloat16 [1024, 8192], P(('context', 'mirror'), 'tensor'), may hold values from -6 to 6
- hyena_v: bfloat16 [1024, 8192], P(('context', 'mirror'), 'tensor'), may hold values from -6 to 6
- filters: bfloat16 [512, 128], P('tensor'), may hold values from -0.5 to 0.5
- norm_gain: float32 [8192], P('tensor'), may hold values from 0.1 to 1.9
- attn_q: bfloat16 [1024, 8192], P(('context', 'mirror'), 'tensor'), may hold values from -35 to 35
- attn_k: bfloat16 [1024, 8192], P(('context', 'mirror'), 'tensor'), may hold values from -5 to 5
- out_grad: bfloat16 [1024, 8192], P(('context', 'mirror'), 'tensor'), may hold values from -20 to 20
- doc_lengths: int32 [4], replicated, may hold values from 1 to 512, 1024 in all
Outputs:
- attn_out: bfloat16 [1024, 8192], P(('context', 'mirror'), 'tensor')
- grad_attn_q: bfloat16 [1024, 8192], P(('context', 'mirror'), 'tensor')
- grad_attn_k: bfloat16 [1024, 8192], P(('context', 'mirror'), 'tensor')
- grad_hyena_q: bfloat16 [1024, 8192], P(('context', 'mirror'), 'tensor')
- grad_hyena_k: bfloat16 [1024, 8192], P(('context', 'mirror'), 'tensor')
- grad_hyena_v: bfloat16 [1024, 8192], P(('context', 'mirror'), 'tensor')
- grad_filters: float32 [512, 128], P('tensor')
The draws below stay inside these ranges and needn't reach their ends.
All inputs are finite; a program needn't handle non-finite values.
Results may differ from the reference program's by a relative error of at most 0.0064.
Values may be sent and summed in bfloat16 or wider, within the bound.
A program may use at most 128 MiB of HBM per device.

```python
import math
import jax
import jax.numpy as jnp
import numpy as np
from jax import lax

HEADS = 64
HEAD = 128
TAPS = 128
D = 8192
GROUP = 16
FILTERS = 512
T_DEV = 128
REACH = 2
DOCS = 4
SEQ = 1024
DOC_MOST = 512


def draw_hyena_q(key, part):
    key_base, key_cols, key_rows = jax.random.split(key, 3)
    col_frac = jnp.arange(D, dtype=jnp.float32) / max(D - 1, 1)
    col_scale = 3.0 ** col_frac * jnp.exp(jax.random.uniform(key_cols, (D,), minval=-0.4, maxval=0.4))
    row_scale = 10.0 ** jax.random.uniform(key_rows, (SEQ,))
    base_draw = jnp.clip(jax.random.normal(key_base, (SEQ, D)), -5.0, 5.0)
    return (base_draw * col_scale[None, :] * row_scale[:, None] / 4.0).astype(jnp.bfloat16)


def drawn_pair(key):
    pair_key = jax.random.fold_in(key, 11)
    key_keys, key_queries = jax.random.split(pair_key)
    key_rows = jnp.clip(jax.random.normal(key_keys, (SEQ, D)), -5.0, 5.0)
    query_rows = jnp.clip(jax.random.normal(key_queries, (SEQ, D)), -5.0, 5.0)
    return (query_rows, key_rows)


def draw_attn_q(key, part):
    return drawn_pair(key)[0].astype(jnp.bfloat16)


def draw_attn_k(key, part):
    return drawn_pair(key)[1].astype(jnp.bfloat16)


def draw_out_grad(key, part):
    key_base, key_rows = jax.random.split(key, 2)
    position_frac = jnp.arange(SEQ, dtype=jnp.float32) / max(SEQ - 1, 1)
    row_scale = 3.0 ** position_frac * 10.0 ** jax.random.uniform(key_rows, (SEQ,)) / 8.0
    base_draw = jnp.clip(jax.random.normal(key_base, (SEQ, D)), -5.0, 5.0)
    return (base_draw * row_scale[:, None]).astype(jnp.bfloat16)


def block_levels(key, extent, cuts, low, largest):
    def one(axis_at, shards_of):
        draws = jax.random.uniform(jax.random.fold_in(jax.random.fold_in(key, 6), axis_at), (shards_of,), jnp.float32, low / len(cuts), largest / len(cuts))
        return jnp.repeat(jnp.exp(draws), extent[axis_at] // shards_of).reshape((-1,) + (1,) * (len(extent) - axis_at - 1))

    level = one(*cuts[0])
    for cut in cuts[1:]:
        level = level * one(*cut)
    return level


def length_profile(amount, total, most, slope):
    portions = [(1 << 20) // math.isqrt(standing ** slope) + 1 for standing in range(2, amount + 1)]
    surplus, holding = total - most - (amount - 1), [1] * (amount - 1)
    while surplus > 0:
        movable = [i for i in range(amount - 1) if holding[i] < most]
        pool, left = sum([portions[i] for i in movable]), surplus
        for i in movable:
            addition = min(most - holding[i], max(1, left * portions[i] // pool), surplus)
            holding[i] = holding[i] + addition
            surplus = surplus - addition
    return np.array([most] + holding)


def uneven(stream_key, count, total, reach, skew):
    if count == 2:
        one = jax.random.randint(stream_key, (), max(1, total - reach), min(reach, total - 1) + 1)
        return jnp.stack([one, total - one])
    tallies = jnp.asarray(length_profile(count, total, reach, skew), jnp.int32)
    twos = (count - 1) // 2
    donor, taker = tallies[1:1 + 2 * twos:2], tallies[2:2 + 2 * twos:2]
    room = jnp.minimum(donor - 1, reach - taker)
    passed = jax.random.randint(jax.random.fold_in(stream_key, 1), (twos,), 0, 1 << 20) % (room + 1)
    tallies = tallies.at[1:1 + 2 * twos:2].set(donor - passed).at[2:2 + 2 * twos:2].set(taker + passed)
    return tallies[jax.random.permutation(jax.random.fold_in(stream_key, 2), count)]


def scatter_about(rng, dims, width, most, cuts=(), kind=jnp.bfloat16):
    values = jax.random.normal(rng, dims, jnp.float32) * width
    if len(cuts) > 0:
        values = block_levels(rng, dims, cuts, -0.22, 0.18) * values
    return jnp.clip(values, min=-most, max=most).astype(kind)


def setup_inputs(seed: int = 0) -> dict:
    arg_keys = jax.random.split(jax.random.key(seed), 10)
    hyena_q = draw_hyena_q(jax.random.fold_in(arg_keys[9], 71), 0)
    hyena_k = scatter_about(arg_keys[1], (SEQ, D), 1.0, 6.0, ((0, 8), (1, 4)))
    hyena_v = scatter_about(arg_keys[2], (SEQ, D), 1.0, 6.0, ((0, 8), (1, 4)))
    filters = scatter_about(arg_keys[3], (FILTERS, TAPS), TAPS ** -0.5, 0.5, ((0, 4),))
    norm_gain = jnp.clip(1.0 + 0.18 * jax.random.normal(arg_keys[4], (D,), jnp.float32), 0.1, 1.9)
    attn_q = draw_attn_q(jax.random.fold_in(arg_keys[9], 71), 0)
    attn_k = draw_attn_k(jax.random.fold_in(arg_keys[9], 71), 0)
    out_grad = draw_out_grad(jax.random.fold_in(arg_keys[9], 71), 0)
    doc_lengths = uneven(arg_keys[8], DOCS, SEQ, DOC_MOST, 2).astype(jnp.int32)
    return {"hyena_q": hyena_q, "hyena_k": hyena_k, "hyena_v": hyena_v, "filters": filters, "norm_gain": norm_gain, "attn_q": attn_q, "attn_k": attn_k, "out_grad": out_grad, "doc_lengths": doc_lengths}


def doc_index(doc_lengths, positions):
    doc_ends = jnp.cumsum(doc_lengths, dtype=jnp.int32)
    return lax.optimization_barrier(jnp.sum((positions[:, None] >= doc_ends[None, :]).astype(jnp.int32), axis=1, dtype=jnp.int32))

def forward_conv(wide_rows, filt_rows, doc_ids):
    width_rows = wide_rows.shape[0]
    padded = jnp.concatenate([jnp.zeros((width_rows, TAPS - 1), jnp.float32), wide_rows], axis=1)
    doc_pad = jnp.concatenate([jnp.full((TAPS - 1,), -1, jnp.int32), doc_ids])

    def tap_step(running, tap_index):
        shifted = lax.dynamic_slice_in_dim(padded, TAPS - 1 - tap_index, SEQ, 1)
        same_doc = lax.dynamic_slice_in_dim(doc_pad, TAPS - 1 - tap_index, SEQ, 0) == doc_ids
        tap_weight = lax.dynamic_slice_in_dim(filt_rows, tap_index, 1, 1)
        return (running + tap_weight * jnp.where(same_doc[None, :], shifted, 0.0), None)
    running, _ = lax.scan(tap_step, jnp.zeros_like(wide_rows), jnp.arange(TAPS, dtype=jnp.int32))
    return running

def backward_conv(grad_rows, wide_rows, filt_rows, doc_ids):
    width_rows = grad_rows.shape[0]
    grad_ahead = jnp.concatenate([grad_rows, jnp.zeros((width_rows, TAPS - 1), jnp.float32)], axis=1)
    doc_ahead = jnp.concatenate([doc_ids, jnp.full((TAPS - 1,), -1, jnp.int32)])
    behind = jnp.concatenate([jnp.zeros((width_rows, TAPS - 1), jnp.float32), wide_rows], axis=1)
    doc_behind = jnp.concatenate([jnp.full((TAPS - 1,), -1, jnp.int32), doc_ids])

    def tap_step(running, tap_index):
        shifted = lax.dynamic_slice_in_dim(grad_ahead, tap_index, SEQ, 1)
        same_doc = lax.dynamic_slice_in_dim(doc_ahead, tap_index, SEQ, 0) == doc_ids
        tap_weight = lax.dynamic_slice_in_dim(filt_rows, tap_index, 1, 1)
        running = running + tap_weight * jnp.where(same_doc[None, :], shifted, 0.0)
        earlier = lax.dynamic_slice_in_dim(behind, TAPS - 1 - tap_index, SEQ, 1)
        same_past = lax.dynamic_slice_in_dim(doc_behind, TAPS - 1 - tap_index, SEQ, 0) == doc_ids
        tap_corr = lax.optimization_barrier(jnp.sum(grad_rows * jnp.where(same_past[None, :], earlier, 0.0), axis=1))
        return (running, tap_corr)
    running, tap_corr = lax.scan(tap_step, jnp.zeros_like(grad_rows), jnp.arange(TAPS, dtype=jnp.int32))
    return (running, tap_corr.T)

def head_pass(query_all, key_all, value_all, grad_all, doc_ids):
    window = (REACH + 1) * T_DEV
    front = REACH * T_DEV
    score_scale = HEAD ** (-0.5)
    key_pad = jnp.concatenate([jnp.zeros((front, HEAD), jnp.bfloat16), key_all], axis=0)
    value_pad = jnp.concatenate([jnp.zeros((front, HEAD), jnp.bfloat16), value_all], axis=0)
    doc_pad = jnp.concatenate([jnp.full((front,), -1, jnp.int32), doc_ids])

    def block_step(carry, block_index):
        key_acc, value_acc = carry
        row_start = (block_index * T_DEV).astype(jnp.int32)
        query_block = lax.dynamic_slice_in_dim(query_all, row_start, T_DEV, 0)
        grad_block = lax.dynamic_slice_in_dim(grad_all, row_start, T_DEV, 0)
        query_doc = lax.dynamic_slice_in_dim(doc_ids, row_start, T_DEV, 0)
        key_block = lax.dynamic_slice_in_dim(key_pad, row_start, window, 0)
        value_block = lax.dynamic_slice_in_dim(value_pad, row_start, window, 0)
        key_doc = lax.dynamic_slice_in_dim(doc_pad, row_start, window, 0)
        query_pos = row_start + jnp.arange(T_DEV, dtype=jnp.int32)
        key_pos = row_start - front + jnp.arange(window, dtype=jnp.int32)
        allowed = (key_pos[None, :] <= query_pos[:, None]) & (query_pos[:, None] - key_pos[None, :] <= front) & (key_doc[None, :] == query_doc[:, None])
        scores = jnp.dot(query_block, key_block.T, preferred_element_type=jnp.float32) * score_scale
        row_top = lax.optimization_barrier(jnp.max(jnp.where(allowed, scores, -1e+30), axis=1, keepdims=True))
        row_total = lax.optimization_barrier(jnp.sum(jnp.exp(jnp.where(allowed, scores - row_top, -1e+30)), axis=1, keepdims=True))
        row_lse = row_top + jnp.log(row_total)
        prob = jnp.where(allowed, jnp.exp(scores - row_lse), 0.0)
        prob_half = prob.astype(jnp.bfloat16)
        out_block = jnp.dot(prob_half, value_block, preferred_element_type=jnp.float32).astype(jnp.bfloat16)
        grad_prob = jnp.dot(grad_block, value_block.T, preferred_element_type=jnp.float32)
        row_delta = lax.optimization_barrier(jnp.sum(prob * grad_prob, axis=1, keepdims=True))
        grad_score = (prob * (grad_prob - row_delta) * score_scale).astype(jnp.bfloat16)
        grad_query = jnp.dot(grad_score, key_block, preferred_element_type=jnp.float32).astype(jnp.bfloat16)
        key_part = jnp.dot(grad_score.T, query_block, preferred_element_type=jnp.float32)
        value_part = jnp.dot(prob_half.T, grad_block, preferred_element_type=jnp.float32)
        key_acc = lax.dynamic_update_slice_in_dim(key_acc, lax.dynamic_slice_in_dim(key_acc, row_start, window, 0) + key_part, row_start, 0)
        value_acc = lax.dynamic_update_slice_in_dim(value_acc, lax.dynamic_slice_in_dim(value_acc, row_start, window, 0) + value_part, row_start, 0)
        return ((key_acc, value_acc), (out_block, grad_query))
    start_acc = jnp.zeros((front + SEQ, HEAD), jnp.float32)
    (key_acc, value_acc), (out_blocks, query_blocks) = lax.scan(block_step, (start_acc, start_acc), jnp.arange(SEQ // T_DEV, dtype=jnp.int32))
    return (out_blocks.reshape(SEQ, HEAD), query_blocks.reshape(SEQ, HEAD), key_acc[front:], value_acc[front:])

def reference(hyena_q, hyena_k, hyena_v, filters, norm_gain, attn_q, attn_k, out_grad, doc_lengths):
    doc_ids = doc_index(doc_lengths, jnp.arange(SEQ, dtype=jnp.int32))
    block_size = min(D, 1024)
    block_count = D // block_size

    def to_blocks(array):
        return array.astype(jnp.float32).T.reshape(block_count, block_size, SEQ)

    def from_blocks(array):
        return array.reshape(D, SEQ).T
    filt_rows = jnp.repeat(filters.astype(jnp.float32), GROUP, axis=0).reshape(block_count, block_size, TAPS)
    kv_product = (hyena_k.astype(jnp.float32) * hyena_v.astype(jnp.float32)).astype(jnp.bfloat16)

    def conv_block(pieces):
        return forward_conv(pieces[0], pieces[1], doc_ids)
    signal = from_blocks(lax.map(conv_block, (to_blocks(kv_product), filt_rows)))
    hyena_mix = hyena_q.astype(jnp.float32) * signal
    inv_rms = lax.rsqrt(lax.optimization_barrier(jnp.sum(hyena_mix * hyena_mix, axis=1)) / D + 1e-06)
    values = (hyena_mix * inv_rms[:, None] * norm_gain[None, :]).astype(jnp.bfloat16)

    def to_heads(array):
        return array.reshape(SEQ, HEADS, HEAD).transpose(1, 0, 2)

    def from_heads(array):
        return array.transpose(1, 0, 2).reshape(SEQ, D)

    def attend_head(pieces):
        return head_pass(pieces[0], pieces[1], pieces[2], pieces[3], doc_ids)
    out_heads, query_heads, key_heads, value_heads = lax.map(attend_head, (to_heads(attn_q), to_heads(attn_k), to_heads(values), to_heads(out_grad)))
    attn_out = from_heads(out_heads)
    grad_attn_q = from_heads(query_heads)
    grad_attn_k = from_heads(key_heads).astype(jnp.bfloat16)
    grad_values = from_heads(value_heads)
    inner_sum = lax.optimization_barrier(jnp.sum(norm_gain[None, :] * grad_values * hyena_mix, axis=1))
    grad_mix = inv_rms[:, None] * (norm_gain[None, :] * grad_values - hyena_mix * (inner_sum * inv_rms * inv_rms / D)[:, None])
    grad_hyena_q = (grad_mix * signal).astype(jnp.bfloat16)
    grad_signal = (grad_mix * hyena_q.astype(jnp.float32)).astype(jnp.bfloat16)

    def back_block(pieces):
        return backward_conv(pieces[0], pieces[1], pieces[2], doc_ids)
    grad_kv, tap_corr = lax.map(back_block, (to_blocks(grad_signal), to_blocks(kv_product), filt_rows))
    grad_kv = from_blocks(grad_kv)
    grad_hyena_k = (grad_kv * hyena_v.astype(jnp.float32)).astype(jnp.bfloat16)
    grad_hyena_v = (grad_kv * hyena_k.astype(jnp.float32)).astype(jnp.bfloat16)
    grad_filters = lax.optimization_barrier(jnp.sum(tap_corr.reshape(D // GROUP, GROUP, TAPS), axis=1))
    return (attn_out, grad_attn_q, grad_attn_k, grad_hyena_q, grad_hyena_k, grad_hyena_v, grad_filters)
```

```python
import functools

import jax
import jax.numpy as jnp
from jax import lax
from jax.experimental import pallas as pl
from jax.experimental.pallas import tpu as pltpu
from jax.sharding import PartitionSpec as P

HEAD = 128
LANES = 128
D = 8192
REACH = 2
NEG = -1e30
MESH = pl.DeviceIdType.MESH
F32 = jnp.float32
BF16 = jnp.bfloat16

KV, K2, K1, Q2, Q1, D2, D1, L1, L2, V2, V1, E1, E2, GS = range(14)
FIXED = 14


def dot_nt(a, b):
    return lax.dot_general(a, b, (((1,), (1,)), ((), ())), preferred_element_type=F32)


def dot_nn(a, b):
    return lax.dot_general(a, b, (((1,), (0,)), ((), ())), preferred_element_type=F32)


def kernel(
    dims,
    hq, hk, hv, filt, filt_rev, gain, aq, ak, og, lens,
    out, gq, gk, ghq, ghk, ghv, gfilt,
    kvwin, gswin, kwin, vwin, qwin, dwin, lrow, erow, prob, prob_t,
    qbias, kbias, fmask, bmask, rmask, signal, gval, cols, stat_out, stat_in,
    gflat, gpart, gin, gsum, send, recv,
):
    contexts, mirrors, tensors = dims
    count = contexts * mirrors
    rows, channels = hq.shape
    groups, taps = filt.shape
    width = channels // groups
    per = LANES // width
    blocks = channels // LANES
    heads = channels // HEAD
    subs = rows // taps
    scale = HEAD ** (-0.5)
    ctx = lax.axis_index("context")
    mir = lax.axis_index("mirror")
    ten = lax.axis_index("tensor")
    me = ctx * mirrors + mir
    base = me * rows

    def token(index):
        index = lax.rem(index + 2 * count, count)
        return {"context": index // mirrors, "mirror": lax.rem(index, mirrors)}

    def peer(index):
        return {"tensor": lax.rem(index, tensors)}

    barrier = pltpu.get_barrier_semaphore()
    for d in range(1, count):
        pl.semaphore_signal(barrier, inc=1, device_id=token(me + d), device_id_type=MESH)
    for d in range(1, tensors):
        pl.semaphore_signal(barrier, inc=1, device_id=peer(ten + d), device_id_type=MESH)
    pl.semaphore_wait(barrier, count - 1 + tensors - 1)

    def copy(slot, src, dst, device):
        return pltpu.make_async_remote_copy(
            src_ref=src, dst_ref=dst, send_sem=send.at[slot], recv_sem=recv.at[slot],
            device_id=device, device_id_type=MESH,
        )

    first, last = ctx == 0, ctx == contexts - 1
    inner_lo, inner_hi = jnp.logical_not(first), jnp.logical_not(last)
    core0, core1 = mir == 0, mir == 1
    partner = token(me + 1 - 2 * mir)
    far, mid, near = pl.ds(0, rows), pl.ds(rows, rows), pl.ds(2 * rows, rows)

    own_tail = pl.ds(rows, taps)
    c_kv = copy(KV, kvwin.at[own_tail], kvwin.at[pl.ds(0, taps)], token(me + 1))
    c_gs = copy(GS, gswin.at[pl.ds(0, taps)], gswin.at[pl.ds(rows, taps)], token(me - 1))
    has_lo, has_hi = me > 0, me < count - 1

    def forward(slot2, slot1, win):
        c2 = copy(slot2, win.at[near], win.at[far], token(me + 2))
        c1_own = copy(slot1, win.at[near], win.at[mid], partner)
        c1_relay = copy(slot1, win.at[far], win.at[mid], partner)
        return c2, c1_own, c1_relay

    def backward(slot2, slot1, win):
        c2 = copy(slot2, win.at[far], win.at[near], token(me - 2))
        c1_own = copy(slot1, win.at[far], win.at[mid], partner)
        c1_relay = copy(slot1, win.at[near], win.at[mid], partner)
        return c2, c1_own, c1_relay

    k_cp = forward(K2, K1, kwin)
    v_cp = forward(V2, V1, vwin)
    q_cp = backward(Q2, Q1, qwin)
    d_cp = backward(D2, D1, dwin)

    def rows_back(slot1, slot2, ref):
        return (
            copy(slot1, ref.at[0], ref.at[1], token(me - 1)),
            copy(slot2, ref.at[0], ref.at[2], token(me - 2)),
        )

    l_cp = rows_back(L1, L2, lrow)
    e_cp = rows_back(E1, E2, erow)

    def when(cond, fn):
        pl.when(cond)(fn)

    def start_forward(cps):
        when(inner_hi, cps[0].start)
        when(core0, cps[1].start)

    def start_backward(cps):
        when(inner_lo, cps[0].start)
        when(core1, cps[1].start)

    def land_forward(cps):
        when(inner_lo, cps[0].wait_recv)
        when(jnp.logical_and(core1, inner_lo), cps[2].start)

    def land_backward(cps):
        when(inner_hi, cps[0].wait_recv)
        when(jnp.logical_and(core0, inner_hi), cps[2].start)

    def finish_forward(cps):
        when(jnp.logical_or(core1, inner_lo), cps[1].wait_recv)

    def finish_backward(cps):
        when(jnp.logical_or(core0, inner_hi), cps[1].wait_recv)

    def drain_forward(cps):
        when(inner_hi, cps[0].wait_send)
        when(core0, cps[1].wait_send)
        when(jnp.logical_and(core1, inner_lo), cps[2].wait_send)

    def drain_backward(cps):
        when(inner_lo, cps[0].wait_send)
        when(core1, cps[1].wait_send)
        when(jnp.logical_and(core0, inner_hi), cps[2].wait_send)

    qwin[far] = aq[...]
    start_backward(q_cp)
    kvwin[pl.ds(taps, rows)] = (hk[...].astype(F32) * hv[...].astype(F32)).astype(BF16)
    when(has_hi, c_kv.start)
    kwin[near] = ak[...]
    start_forward(k_cp)
    dwin[far] = og[...]
    start_backward(d_cp)

    def zero(ref, at):
        ref[at] = jnp.zeros((ref[at].shape), ref.dtype)

    when(me == 0, lambda: zero(kvwin, pl.ds(0, taps)))
    when(me == count - 1, lambda: zero(gswin, pl.ds(rows, taps)))
    when(first, lambda: zero(kwin, far))
    when(first, lambda: zero(vwin, far))
    when(me == 0, lambda: zero(kwin, mid))
    when(me == 0, lambda: zero(vwin, mid))
    when(last, lambda: zero(qwin, near))
    when(last, lambda: zero(dwin, near))
    when(me == count - 1, lambda: zero(qwin, mid))
    when(me == count - 1, lambda: zero(dwin, mid))
    when(me == count - 1, lambda: zero(lrow, 1))
    when(me == count - 1, lambda: zero(erow, 1))
    when(me >= count - 2, lambda: zero(lrow, 2))
    when(me >= count - 2, lambda: zero(erow, 2))

    ends = []
    total = jnp.int32(0)
    for i in range(lens.shape[0]):
        total = total + lens[i]
        ends.append(total)

    def doc(pos):
        return sum((pos >= e).astype(jnp.int32) for e in ends)

    def grid(shape, row0, col0):
        return (
            row0 + lax.broadcasted_iota(jnp.int32, shape, 0),
            col0 + lax.broadcasted_iota(jnp.int32, shape, 1),
        )

    t_pos, u_pos = grid((rows, 3 * rows), base, base - 2 * rows)
    ok = (u_pos >= 0) & (u_pos <= t_pos) & (t_pos - u_pos <= REACH * rows) & (doc(u_pos) == doc(t_pos))
    qbias[...] = jnp.where(ok, 0.0, NEG)
    u_pos, t_pos = grid((rows, 3 * rows), base, base)
    ok = (u_pos <= t_pos) & (t_pos - u_pos <= REACH * rows) & (doc(u_pos) == doc(t_pos))
    kbias[...] = jnp.where(ok, 0.0, NEG)
    for s in range(subs):
        at = pl.ds(s * taps, taps)
        t_pos, u_pos = grid((taps, 2 * taps), base + s * taps, base + (s - 1) * taps)
        ok = (u_pos >= 0) & (u_pos <= t_pos) & (t_pos - u_pos < taps) & (doc(u_pos) == doc(t_pos))
        fmask[at] = jnp.where(ok, 1.0, 0.0).astype(BF16)
        halves = []
        for i in range(2):
            t_pos, w_pos = grid((taps, taps), base + s * taps, 0)
            u_pos = base + (s - 1 + i) * taps + lax.rem(taps - w_pos, taps)
            ok = (u_pos >= 0) & (u_pos <= t_pos) & (t_pos - u_pos < taps) & (doc(u_pos) == doc(t_pos))
            halves.append(jnp.where(ok, 1.0, 0.0))
        rmask[at] = jnp.concatenate(halves, axis=1)
        t_pos, u_pos = grid((taps, 2 * taps), base + s * taps, base + s * taps)
        ok = (u_pos >= t_pos) & (u_pos - t_pos < taps) & (doc(u_pos) == doc(t_pos))
        bmask[at] = jnp.where(ok, 1.0, 0.0).astype(BF16)

    lane = lax.broadcasted_iota(jnp.int32, (taps, LANES), 1)

    def chan(b):
        return pl.ds(pl.multiple_of(b * LANES, LANES), LANES)

    def toeplitz(ref, b):
        made = []
        for i in range(per):
            row = jnp.broadcast_to(ref[pl.ds(b * per + i, 1), :], (taps, taps))
            made.append(pltpu.roll(row, 0, 1, stride=1, stride_axis=0).astype(BF16))
        return made

    def conv(bands, mask, window):
        mask_lo, mask_hi = mask[:, :taps], mask[:, taps:]
        stack = jnp.concatenate(
            [jnp.concatenate([band * mask_lo, band * mask_hi], axis=1) for band in bands], axis=0
        )
        every = dot_nn(stack, window)
        picked = every[:taps]
        for i in range(1, per):
            picked = jnp.where(lane >= i * width, every[i * taps : (i + 1) * taps], picked)
        return picked

    when(has_lo, c_kv.wait_recv)

    def signal_step(b, acc):
        at = chan(b)
        bands = toeplitz(filt_rev, b)
        parts = []
        for s in range(subs):
            here = pl.ds(s * taps, taps)
            made = conv(bands, fmask[here], kvwin[pl.ds(s * taps, 2 * taps), at])
            signal[here, at] = made
            mix = hq[here, at].astype(F32) * made
            parts.append(mix * mix)
        return acc + jnp.concatenate(parts, axis=0)

    squares = lax.fori_loop(0, blocks, signal_step, jnp.zeros((rows, LANES), F32))

    land_forward(k_cp)
    finish_forward(k_cp)
    col_lane = lax.broadcasted_iota(jnp.int32, (rows, LANES), 1)

    def lse_step(h, acc):
        at = chan(h)
        score = dot_nt(aq[:, at], kwin[:, at]) * scale + qbias[...]
        top = jnp.max(score, axis=1, keepdims=True)
        lse = top + jnp.log(jnp.sum(jnp.exp(score - top), axis=1, keepdims=True))
        prob[h] = jnp.exp(score - lse)
        return jnp.where(col_lane == h, lse, acc)

    cols[...] = lax.fori_loop(0, heads, lse_step, jnp.zeros((rows, LANES), F32))
    lrow[0] = jnp.transpose(cols[...])[:heads]
    when(me > 0, l_cp[0].start)
    when(me > 1, l_cp[1].start)

    land_backward(q_cp)
    land_backward(d_cp)
    finish_backward(q_cp)
    finish_backward(d_cp)
    when(me < count - 1, l_cp[0].wait_recv)
    when(me < count - 2, l_cp[1].wait_recv)

    def wide_row(ref, h):
        return jnp.concatenate([ref[j, pl.ds(h, 1), :] for j in range(3)], axis=1)

    def gval_step(h, acc):
        at = chan(h)
        score = dot_nt(ak[:, at], qwin[:, at]) * scale + kbias[...]
        p = jnp.exp(score - wide_row(lrow, h))
        prob_t[h] = p
        made = dot_nn(p.astype(BF16), dwin[:, at])
        gval[:, at] = made
        return acc + gain[:, at] * made * (hq[:, at].astype(F32) * signal[:, at])

    inner = lax.fori_loop(0, heads, gval_step, jnp.zeros((rows, LANES), F32))

    cols[...] = jnp.where(
        col_lane == 0,
        jnp.sum(squares, axis=1, keepdims=True),
        jnp.where(col_lane == 1, jnp.sum(inner, axis=1, keepdims=True), 0.0),
    )
    stat_out[...] = jnp.transpose(cols[...])[:8]
    stat_cp = [
        copy(FIXED + d - 1, stat_out, stat_in.at[d - 1], peer(ten + d)) for d in range(1, tensors)
    ]
    for c in stat_cp:
        c.start()
    for c in stat_cp:
        c.wait_recv()
    stats = stat_out[...]
    for d in range(1, tensors):
        stats = stats + stat_in[d - 1]
    stats = jnp.transpose(jnp.concatenate([stats, jnp.zeros((LANES - 8, rows), F32)], axis=0))
    inv = lax.rsqrt(stats[:, 0:1] / D + 1e-06)
    pull = stats[:, 1:2] * inv * inv / D

    def norm_step(b, carry):
        at = chan(b)
        gate = hq[:, at].astype(F32)
        made = signal[:, at]
        mix = gate * made
        gains = gain[:, at]
        vwin[near, at] = (mix * inv * gains).astype(BF16)
        grad_mix = inv * (gains * gval[:, at] - mix * pull)
        ghq[:, at] = (grad_mix * made).astype(BF16)
        gswin[pl.ds(0, rows), at] = (grad_mix * gate).astype(BF16)
        return carry

    lax.fori_loop(0, blocks, norm_step, 0)
    when(has_lo, c_gs.start)
    start_forward(v_cp)

    row_at, col_at = grid((taps, taps), 0, 0)
    turn = jnp.where(lax.rem(row_at + col_at, taps) == 0, 1.0, 0.0).astype(BF16)

    def filter_step(b, carry):
        at = chan(b)
        sums = [jnp.zeros((1, taps), F32) for _ in range(per)]
        for s in range(subs):
            grads = gswin[pl.ds(s * taps, taps), at]
            stack = jnp.concatenate(
                [
                    jnp.where((lane >= i * width) & (lane < (i + 1) * width), grads, jnp.zeros_like(grads))
                    for i in range(per)
                ],
                axis=0,
            )
            turned = jnp.concatenate(
                [
                    dot_nn(turn, kvwin[pl.ds((s + i) * taps, taps), at]).astype(BF16)
                    for i in range(2)
                ],
                axis=0,
            )
            every = dot_nt(stack, turned)
            mask = rmask[pl.ds(s * taps, taps)]
            for i in range(per):
                part = every[i * taps : (i + 1) * taps] * mask
                part = part[:, :taps] + part[:, taps:]
                part = pltpu.roll(part, 0, 1, stride=1, stride_axis=0)
                sums[i] = sums[i] + jnp.sum(part, axis=0, keepdims=True)
        gflat[pl.ds(pl.multiple_of(b * per, per), per), :] = jnp.concatenate(sums, axis=0)
        return carry

    lax.fori_loop(0, blocks, filter_step, 0)
    share = groups // count
    for i in range(count):
        gpart[i] = gflat[i * share : (i + 1) * share]
    at0 = FIXED + tensors - 1
    scatter = [
        copy(at0 + d - 1, gpart.at[lax.rem(me + d, count)], gin.at[d - 1], token(me + d))
        for d in range(1, count)
    ]
    for c in scatter:
        c.start()

    when(has_hi, c_gs.wait_recv)

    def back_step(b, carry):
        at = chan(b)
        bands = toeplitz(filt, b)
        for s in range(subs):
            here = pl.ds(s * taps, taps)
            made = conv(bands, bmask[here], gswin[pl.ds(s * taps, 2 * taps), at])
            ghk[here, at] = (made * hv[here, at].astype(F32)).astype(BF16)
            ghv[here, at] = (made * hk[here, at].astype(F32)).astype(BF16)
        return carry

    lax.fori_loop(0, blocks, back_step, 0)

    for c in scatter:
        c.wait_recv()
    mine = gpart[me]
    for d in range(1, count):
        mine = mine + gin[d - 1]
    gsum[me] = mine
    at1 = at0 + count - 1
    gather = [
        copy(at1 + d - 1, gsum.at[me], gsum.at[me], token(me + d)) for d in range(1, count)
    ]
    for c in gather:
        c.start()

    land_forward(v_cp)
    finish_forward(v_cp)

    def query_step(h, acc):
        at = chan(h)
        values = vwin[:, at]
        p = prob[h]
        grad_p = dot_nt(og[:, at], values)
        out[:, at] = dot_nn(p.astype(BF16), values).astype(BF16)
        delta = jnp.sum(p * grad_p, axis=1, keepdims=True)
        ds = (p * (grad_p - delta) * scale).astype(BF16)
        gq[:, at] = dot_nn(ds, kwin[:, at]).astype(BF16)
        return jnp.where(col_lane == h, delta, acc)

    cols[...] = lax.fori_loop(0, heads, query_step, jnp.zeros((rows, LANES), F32))
    erow[0] = jnp.transpose(cols[...])[:heads]
    when(me > 0, e_cp[0].start)
    when(me > 1, e_cp[1].start)

    for d in range(1, count):
        other = lax.rem(me - d + count, count)
        copy(at1 + d - 1, gsum.at[other], gsum.at[other], token(me + d)).wait_recv()
    for i in range(count):
        gfilt[i * share : (i + 1) * share] = gsum[i]

    when(me < count - 1, e_cp[0].wait_recv)
    when(me < count - 2, e_cp[1].wait_recv)

    def key_step(h, carry):
        at = chan(h)
        grad_p = dot_nt(vwin[near, at], dwin[:, at])
        ds = (prob_t[h] * (grad_p - wide_row(erow, h)) * scale).astype(BF16)
        gk[:, at] = dot_nn(ds, qwin[:, at]).astype(BF16)
        return carry

    lax.fori_loop(0, heads, key_step, 0)

    when(has_hi, c_kv.wait_send)
    when(has_lo, c_gs.wait_send)
    drain_forward(k_cp)
    drain_forward(v_cp)
    drain_backward(q_cp)
    drain_backward(d_cp)
    for cps in (l_cp, e_cp):
        when(me > 0, cps[0].wait_send)
        when(me > 1, cps[1].wait_send)
    for c in stat_cp + scatter + gather:
        c.wait_send()


def body(dims, hyena_q, hyena_k, hyena_v, filters, norm_gain, attn_q, attn_k, out_grad, doc_lengths):
    contexts, mirrors, tensors = dims
    count = contexts * mirrors
    rows, channels = hyena_q.shape
    groups, taps = filters.shape
    heads = channels // HEAD
    share = groups // count
    filt = filters.astype(F32)
    filt_rev = jnp.concatenate([filt[:, :1], filt[:, :0:-1]], axis=1)
    slots = FIXED + tensors - 1 + 2 * (count - 1)
    window = (3 * rows, channels)
    tile = jax.ShapeDtypeStruct((rows, channels), BF16)
    vmem = pl.BlockSpec(memory_space=pltpu.VMEM)
    results = pl.pallas_call(
        functools.partial(kernel, dims),
        out_shape=(tile,) * 6 + (jax.ShapeDtypeStruct((groups, taps), F32),),
        in_specs=[vmem] * 9 + [pl.BlockSpec(memory_space=pltpu.SMEM)],
        out_specs=(vmem,) * 7,
        scratch_shapes=[
            pltpu.VMEM((taps + rows, channels), BF16),
            pltpu.VMEM((taps + rows, channels), BF16),
            pltpu.VMEM(window, BF16),
            pltpu.VMEM(window, BF16),
            pltpu.VMEM(window, BF16),
            pltpu.VMEM(window, BF16),
            pltpu.VMEM((3, heads, rows), F32),
            pltpu.VMEM((3, heads, rows), F32),
            pltpu.VMEM((heads, rows, 3 * rows), F32),
            pltpu.VMEM((heads, rows, 3 * rows), F32),
            pltpu.VMEM((rows, 3 * rows), F32),
            pltpu.VMEM((rows, 3 * rows), F32),
            pltpu.VMEM((rows, 2 * taps), BF16),
            pltpu.VMEM((rows, 2 * taps), BF16),
            pltpu.VMEM((rows, 2 * taps), F32),
            pltpu.VMEM((rows, channels), F32),
            pltpu.VMEM((rows, channels), F32),
            pltpu.VMEM((rows, LANES), F32),
            pltpu.VMEM((8, rows), F32),
            pltpu.VMEM((tensors - 1, 8, rows), F32),
            pltpu.VMEM((groups, taps), F32),
            pltpu.VMEM((count, share, taps), F32),
            pltpu.VMEM((count - 1, share, taps), F32),
            pltpu.VMEM((count, share, taps), F32),
            pltpu.SemaphoreType.DMA((slots,)),
            pltpu.SemaphoreType.DMA((slots,)),
        ],
        compiler_params=pltpu.CompilerParams(
            collective_id=0, has_side_effects=True, vmem_limit_bytes=63 * 1024 * 1024
        ),
        name="hyena_attention",
    )(
        hyena_q, hyena_k, hyena_v, filt, filt_rev, norm_gain[None, :], attn_q, attn_k, out_grad,
        doc_lengths,
    )
    return results


def solution(mesh):
    dims = (mesh.shape["context"], mesh.shape["mirror"], mesh.shape["tensor"])
    tokens = P(("context", "mirror"), "tensor")
    return jax.shard_map(
        functools.partial(body, dims),
        mesh=mesh,
        in_specs=(tokens, tokens, tokens, P("tensor", None), P("tensor"), tokens, tokens, tokens, P()),
        out_specs=(tokens,) * 6 + (P("tensor", None),),
        check_vma=False,
    )
```

```python
import functools

import jax
import jax.numpy as jnp
from jax import lax
from jax.experimental import pallas as pl
from jax.experimental.pallas import tpu as pltpu
from jax.sharding import PartitionSpec as P

HEAD = 128
LANES = 128
D = 8192
REACH = 2
NEG = -1e30
MESH = pl.DeviceIdType.MESH
F32 = jnp.float32
BF16 = jnp.bfloat16

CHUNKS = 2
KV, K2, K1, Q2, Q1, D2, D1, L1, L2, V2, V1, E1, E2, GS = range(14)
FIXED = 14 * CHUNKS


def dot_nt(a, b):
    return lax.dot_general(a, b, (((1,), (1,)), ((), ())), preferred_element_type=F32)


def dot_nn(a, b):
    return lax.dot_general(a, b, (((1,), (0,)), ((), ())), preferred_element_type=F32)


def kernel(
    dims,
    hq, hk, hv, filt_in, gain, aq, ak, og, lens,
    out, gq, gk, ghq, ghk, ghv, gfilt,
    filt, filt_rev, kvwin, gswin, kwin, vwin, qwin, dwin, lrow, erow, prob, prob_t,
    qbias, kbias, fmask, bmask, rmask, signal, gval, cols, stat_out, stat_in,
    gflat, gpart, gin, gsum, send, recv,
):
    contexts, mirrors, tensors = dims
    count = contexts * mirrors
    rows, channels = hq.shape
    groups, taps = filt_in.shape
    width = channels // groups
    per = LANES // width
    blocks = channels // LANES
    heads = channels // HEAD
    subs = rows // taps
    scale = HEAD ** (-0.5)
    ctx = lax.axis_index("context")
    mir = lax.axis_index("mirror")
    ten = lax.axis_index("tensor")
    me = ctx * mirrors + mir
    base = me * rows

    def token(index):
        index = lax.rem(index + 2 * count, count)
        return {"context": index // mirrors, "mirror": lax.rem(index, mirrors)}

    def peer(index):
        return {"tensor": lax.rem(index, tensors)}

    barrier = pltpu.get_barrier_semaphore()
    for d in range(1, count):
        pl.semaphore_signal(barrier, inc=1, device_id=token(me + d), device_id_type=MESH)
    for d in range(1, tensors):
        pl.semaphore_signal(barrier, inc=1, device_id=peer(ten + d), device_id_type=MESH)
    pl.semaphore_wait(barrier, count - 1 + tensors - 1)

    def copy(slot, src, dst, device):
        return pltpu.make_async_remote_copy(
            src_ref=src, dst_ref=dst, send_sem=send.at[slot], recv_sem=recv.at[slot],
            device_id=device, device_id_type=MESH,
        )

    first, last = ctx == 0, ctx == contexts - 1
    inner_lo, inner_hi = jnp.logical_not(first), jnp.logical_not(last)
    core0, core1 = mir == 0, mir == 1
    partner = token(me + 1 - 2 * mir)
    far, mid, near = pl.ds(0, rows), pl.ds(rows, rows), pl.ds(2 * rows, rows)

    span = channels // CHUNKS
    own_tail = pl.ds(rows, taps)
    has_lo, has_hi = me > 0, me < count - 1

    def cut(c):
        return pl.ds(c * span, span)

    def chunked(slot, src, src_rows, dst, dst_rows, device):
        return [
            copy(slot * CHUNKS + c, src.at[src_rows, cut(c)], dst.at[dst_rows, cut(c)], device)
            for c in range(CHUNKS)
        ]

    c_kv = chunked(KV, kvwin, own_tail, kvwin, pl.ds(0, taps), token(me + 1))
    c_gs = chunked(GS, gswin, pl.ds(0, taps), gswin, pl.ds(rows, taps), token(me - 1))

    def forward(slot2, slot1, win):
        return (
            chunked(slot2, win, near, win, far, token(me + 2)),
            chunked(slot1, win, near, win, mid, partner),
            chunked(slot1, win, far, win, mid, partner),
        )

    def backward(slot2, slot1, win):
        return (
            chunked(slot2, win, far, win, near, token(me - 2)),
            chunked(slot1, win, far, win, mid, partner),
            chunked(slot1, win, near, win, mid, partner),
        )

    k_cp = forward(K2, K1, kwin)
    v_cp = forward(V2, V1, vwin)
    q_cp = backward(Q2, Q1, qwin)
    d_cp = backward(D2, D1, dwin)
    few = heads // CHUNKS

    def rows_back(slot1, slot2, ref):
        def one(slot, to, c, device):
            at = pl.ds(c * few, few)
            return copy(slot * CHUNKS + c, ref.at[0, at], ref.at[to, at], device)

        return (
            [one(slot1, 1, c, token(me - 1)) for c in range(CHUNKS)],
            [one(slot2, 2, c, token(me - 2)) for c in range(CHUNKS)],
        )

    l_cp = rows_back(L1, L2, lrow)
    e_cp = rows_back(E1, E2, erow)

    def when(cond, fn):
        pl.when(cond)(fn)

    def start_forward(cps, c):
        when(inner_hi, cps[0][c].start)
        when(core0, cps[1][c].start)

    def start_backward(cps, c):
        when(inner_lo, cps[0][c].start)
        when(core1, cps[1][c].start)

    def land_forward(cps, c):
        when(inner_lo, cps[0][c].wait_recv)
        when(jnp.logical_and(core1, inner_lo), cps[2][c].start)

    def land_backward(cps, c):
        when(inner_hi, cps[0][c].wait_recv)
        when(jnp.logical_and(core0, inner_hi), cps[2][c].start)

    def finish_forward(cps, c):
        when(jnp.logical_or(core1, inner_lo), cps[1][c].wait_recv)

    def finish_backward(cps, c):
        when(jnp.logical_or(core0, inner_hi), cps[1][c].wait_recv)

    def start_rows(cps, c):
        when(me > 0, cps[0][c].start)
        when(me > 1, cps[1][c].start)

    def finish_rows(cps, c):
        when(me < count - 1, cps[0][c].wait_recv)
        when(me < count - 2, cps[1][c].wait_recv)

    def drain_forward(cps, c):
        when(inner_hi, cps[0][c].wait_send)
        when(core0, cps[1][c].wait_send)
        when(jnp.logical_and(core1, inner_lo), cps[2][c].wait_send)

    def drain_backward(cps, c):
        when(inner_lo, cps[0][c].wait_send)
        when(core1, cps[1][c].wait_send)
        when(jnp.logical_and(core0, inner_hi), cps[2][c].wait_send)

    kwin[near] = ak[...]
    qwin[far] = aq[...]
    dwin[far] = og[...]
    for c in range(CHUNKS):
        start_forward(k_cp, c)
        start_backward(q_cp, c)
        start_backward(d_cp, c)
    kvwin[pl.ds(taps, rows)] = (hk[...].astype(F32) * hv[...].astype(F32)).astype(BF16)
    for c in range(CHUNKS):
        when(has_hi, c_kv[c].start)

    def zero(ref, at):
        ref[at] = jnp.zeros((ref[at].shape), ref.dtype)

    when(me == 0, lambda: zero(kvwin, pl.ds(0, taps)))
    when(me == count - 1, lambda: zero(gswin, pl.ds(rows, taps)))
    when(first, lambda: zero(kwin, far))
    when(first, lambda: zero(vwin, far))
    when(me == 0, lambda: zero(kwin, mid))
    when(me == 0, lambda: zero(vwin, mid))
    when(last, lambda: zero(qwin, near))
    when(last, lambda: zero(dwin, near))
    when(me == count - 1, lambda: zero(qwin, mid))
    when(me == count - 1, lambda: zero(dwin, mid))
    when(me == count - 1, lambda: zero(lrow, 1))
    when(me == count - 1, lambda: zero(erow, 1))
    when(me >= count - 2, lambda: zero(lrow, 2))
    when(me >= count - 2, lambda: zero(erow, 2))

    row_at = lax.broadcasted_iota(jnp.int32, (taps, taps), 0)
    col_at = lax.broadcasted_iota(jnp.int32, (taps, taps), 1)
    turn = jnp.where(lax.rem(row_at + col_at, taps) == 0, 1.0, 0.0).astype(BF16)
    filt[...] = filt_in[...].astype(F32)
    filt_rev[...] = dot_nn(filt_in[...], turn)

    ends = []
    total = jnp.int32(0)
    for i in range(lens.shape[0]):
        total = total + lens[i]
        ends.append(total)

    def doc(pos):
        return sum((pos >= e).astype(jnp.int32) for e in ends)

    def grid(shape, row0, col0):
        return (
            row0 + lax.broadcasted_iota(jnp.int32, shape, 0),
            col0 + lax.broadcasted_iota(jnp.int32, shape, 1),
        )

    t_pos, u_pos = grid((rows, 3 * rows), base, base - 2 * rows)
    ok = (u_pos >= 0) & (u_pos <= t_pos) & (t_pos - u_pos <= REACH * rows) & (doc(u_pos) == doc(t_pos))
    qbias[...] = jnp.where(ok, 0.0, NEG)
    u_pos, t_pos = grid((rows, 3 * rows), base, base)
    ok = (u_pos <= t_pos) & (t_pos - u_pos <= REACH * rows) & (doc(u_pos) == doc(t_pos))
    kbias[...] = jnp.where(ok, 0.0, NEG)
    for s in range(subs):
        at = pl.ds(s * taps, taps)
        t_pos, u_pos = grid((taps, 2 * taps), base + s * taps, base + (s - 1) * taps)
        ok = (u_pos >= 0) & (u_pos <= t_pos) & (t_pos - u_pos < taps) & (doc(u_pos) == doc(t_pos))
        fmask[at] = jnp.where(ok, 1.0, 0.0).astype(BF16)
        halves = []
        for i in range(2):
            t_pos, w_pos = grid((taps, taps), base + s * taps, 0)
            u_pos = base + (s - 1 + i) * taps + lax.rem(taps - w_pos, taps)
            ok = (u_pos >= 0) & (u_pos <= t_pos) & (t_pos - u_pos < taps) & (doc(u_pos) == doc(t_pos))
            halves.append(jnp.where(ok, 1.0, 0.0))
        rmask[at] = jnp.concatenate(halves, axis=1)
        t_pos, u_pos = grid((taps, 2 * taps), base + s * taps, base + s * taps)
        ok = (u_pos >= t_pos) & (u_pos - t_pos < taps) & (doc(u_pos) == doc(t_pos))
        bmask[at] = jnp.where(ok, 1.0, 0.0).astype(BF16)

    lane = lax.broadcasted_iota(jnp.int32, (taps, LANES), 1)

    def chan(b):
        return pl.ds(pl.multiple_of(b * LANES, LANES), LANES)

    def toeplitz(ref, b):
        made = []
        for i in range(per):
            row = jnp.broadcast_to(ref[pl.ds(b * per + i, 1), :], (taps, taps))
            made.append(pltpu.roll(row, 0, 1, stride=1, stride_axis=0).astype(BF16))
        return made

    def conv(bands, mask, window):
        mask_lo, mask_hi = mask[:, :taps], mask[:, taps:]
        stack = jnp.concatenate(
            [jnp.concatenate([band * mask_lo, band * mask_hi], axis=1) for band in bands], axis=0
        )
        every = dot_nn(stack, window)
        picked = every[:taps]
        for i in range(1, per):
            picked = jnp.where(lane >= i * width, every[i * taps : (i + 1) * taps], picked)
        return picked

    def signal_step(b, acc):
        at = chan(b)
        bands = toeplitz(filt_rev, b)
        parts = []
        for s in range(subs):
            here = pl.ds(s * taps, taps)
            made = conv(bands, fmask[here], kvwin[pl.ds(s * taps, 2 * taps), at])
            signal[here, at] = made
            mix = hq[here, at].astype(F32) * made
            parts.append(mix * mix)
        return acc + jnp.concatenate(parts, axis=0)

    col_lane = lax.broadcasted_iota(jnp.int32, (rows, LANES), 1)

    def lse_step(h, acc):
        at = chan(h)
        score = dot_nt(aq[:, at], kwin[:, at]) * scale + qbias[...]
        top = jnp.max(score, axis=1, keepdims=True)
        lse = top + jnp.log(jnp.sum(jnp.exp(score - top), axis=1, keepdims=True))
        prob[h] = jnp.exp(score - lse)
        return jnp.where(col_lane == h, lse, acc)

    zeros = jnp.zeros((rows, LANES), F32)

    def over_heads(step, c, acc, unroll=4):
        return lax.fori_loop(c * few, (c + 1) * few, step, acc, unroll=unroll)

    for c in range(CHUNKS):
        land_forward(k_cp, c)
        finish_forward(k_cp, c)
        cols[...] = over_heads(lse_step, c, zeros)
        lrow[0, c * few : (c + 1) * few] = jnp.transpose(cols[...])[c * few : (c + 1) * few]
        start_rows(l_cp, c)

    def wide_row(ref, h):
        return jnp.concatenate([ref[j, pl.ds(h, 1), :] for j in range(3)], axis=1)

    def gval_step(h, acc):
        at = chan(h)
        score = dot_nt(ak[:, at], qwin[:, at]) * scale + kbias[...]
        p = jnp.exp(score - wide_row(lrow, h))
        prob_t[h] = p
        made = dot_nn(p.astype(BF16), dwin[:, at])
        gval[:, at] = made
        return acc + gain[:, at] * made * (hq[:, at].astype(F32) * signal[:, at])

    squares = inner = zeros
    for c in range(CHUNKS):
        when(has_lo, c_kv[c].wait_recv)
        land_backward(q_cp, c)
        land_backward(d_cp, c)
        squares = over_heads(signal_step, c, squares, 2)
        finish_backward(q_cp, c)
        finish_backward(d_cp, c)
        finish_rows(l_cp, c)
        inner = over_heads(gval_step, c, inner)

    cols[...] = jnp.where(
        col_lane == 0,
        jnp.sum(squares, axis=1, keepdims=True),
        jnp.where(col_lane == 1, jnp.sum(inner, axis=1, keepdims=True), 0.0),
    )
    stat_out[...] = jnp.transpose(cols[...])[:8]
    stat_cp = [
        copy(FIXED + d - 1, stat_out, stat_in.at[d - 1], peer(ten + d)) for d in range(1, tensors)
    ]
    for c in stat_cp:
        c.start()
    for c in stat_cp:
        c.wait_recv()
    stats = stat_out[...]
    for d in range(1, tensors):
        stats = stats + stat_in[d - 1]
    stats = jnp.transpose(jnp.concatenate([stats, jnp.zeros((LANES - 8, rows), F32)], axis=0))
    inv = lax.rsqrt(stats[:, 0:1] / D + 1e-06)
    pull = stats[:, 1:2] * inv * inv / D

    def norm_step(b, carry):
        at = chan(b)
        gate = hq[:, at].astype(F32)
        made = signal[:, at]
        mix = gate * made
        gains = gain[:, at]
        vwin[near, at] = (mix * inv * gains).astype(BF16)
        grad_mix = inv * (gains * gval[:, at] - mix * pull)
        ghq[:, at] = (grad_mix * made).astype(BF16)
        gswin[pl.ds(0, rows), at] = (grad_mix * gate).astype(BF16)
        return carry

    for c in range(CHUNKS):
        over_heads(norm_step, c, 0)
        start_forward(v_cp, c)
        when(has_lo, c_gs[c].start)

    def filter_step(b, carry):
        at = chan(b)
        sums = [jnp.zeros((1, taps), F32) for _ in range(per)]
        for s in range(subs):
            grads = gswin[pl.ds(s * taps, taps), at]
            stack = jnp.concatenate(
                [
                    jnp.where((lane >= i * width) & (lane < (i + 1) * width), grads, jnp.zeros_like(grads))
                    for i in range(per)
                ],
                axis=0,
            )
            turned = jnp.concatenate(
                [
                    dot_nn(turn, kvwin[pl.ds((s + i) * taps, taps), at]).astype(BF16)
                    for i in range(2)
                ],
                axis=0,
            )
            every = dot_nt(stack, turned)
            mask = rmask[pl.ds(s * taps, taps)]
            for i in range(per):
                part = every[i * taps : (i + 1) * taps] * mask
                part = part[:, :taps] + part[:, taps:]
                part = pltpu.roll(part, 0, 1, stride=1, stride_axis=0)
                sums[i] = sums[i] + jnp.sum(part, axis=0, keepdims=True)
        gflat[pl.ds(pl.multiple_of(b * per, per), per), :] = jnp.concatenate(sums, axis=0)
        return carry

    lax.fori_loop(0, blocks, filter_step, 0, unroll=2)
    share = groups // count
    for i in range(count):
        gpart[i] = gflat[i * share : (i + 1) * share]
    at0 = FIXED + tensors - 1
    scatter = [
        copy(at0 + d - 1, gpart.at[lax.rem(me + d, count)], gin.at[d - 1], token(me + d))
        for d in range(1, count)
    ]
    for c in scatter:
        c.start()

    def back_step(b, carry):
        at = chan(b)
        bands = toeplitz(filt, b)
        for s in range(subs):
            here = pl.ds(s * taps, taps)
            made = conv(bands, bmask[here], gswin[pl.ds(s * taps, 2 * taps), at])
            ghk[here, at] = (made * hv[here, at].astype(F32)).astype(BF16)
            ghv[here, at] = (made * hk[here, at].astype(F32)).astype(BF16)
        return carry

    at1 = at0 + count - 1
    gather = [
        copy(at1 + d - 1, gsum.at[me], gsum.at[me], token(me + d)) for d in range(1, count)
    ]

    def query_step(h, acc):
        at = chan(h)
        values = vwin[:, at]
        p = prob[h]
        grad_p = dot_nt(og[:, at], values)
        out[:, at] = dot_nn(p.astype(BF16), values).astype(BF16)
        delta = jnp.sum(p * grad_p, axis=1, keepdims=True)
        ds = (p * (grad_p - delta) * scale).astype(BF16)
        gq[:, at] = dot_nn(ds, kwin[:, at]).astype(BF16)
        return jnp.where(col_lane == h, delta, acc)

    for c in range(CHUNKS):
        when(has_hi, c_gs[c].wait_recv)
        land_forward(v_cp, c)
        over_heads(back_step, c, 0, 2)
        if c == CHUNKS - 1:
            for d in scatter:
                d.wait_recv()
            mine = gpart[me]
            for d in range(1, count):
                mine = mine + gin[d - 1]
            gsum[me] = mine
            for d in gather:
                d.start()
        finish_forward(v_cp, c)
        cols[...] = over_heads(query_step, c, zeros)
        erow[0, c * few : (c + 1) * few] = jnp.transpose(cols[...])[c * few : (c + 1) * few]
        start_rows(e_cp, c)

    for d in range(1, count):
        other = lax.rem(me - d + count, count)
        copy(at1 + d - 1, gsum.at[other], gsum.at[other], token(me + d)).wait_recv()
    for i in range(count):
        gfilt[i * share : (i + 1) * share] = gsum[i]

    def key_step(h, carry):
        at = chan(h)
        grad_p = dot_nt(vwin[near, at], dwin[:, at])
        ds = (prob_t[h] * (grad_p - wide_row(erow, h)) * scale).astype(BF16)
        gk[:, at] = dot_nn(ds, qwin[:, at]).astype(BF16)
        return carry

    for c in range(CHUNKS):
        finish_rows(e_cp, c)
        over_heads(key_step, c, 0)

    for c in range(CHUNKS):
        when(has_hi, c_kv[c].wait_send)
        when(has_lo, c_gs[c].wait_send)
        drain_forward(k_cp, c)
        drain_forward(v_cp, c)
        drain_backward(q_cp, c)
        drain_backward(d_cp, c)
        for cps in (l_cp, e_cp):
            when(me > 0, cps[0][c].wait_send)
            when(me > 1, cps[1][c].wait_send)
    for c in stat_cp + scatter + gather:
        c.wait_send()


def hand_on(*refs):
    count = (len(refs) - 1) // 2
    sems = refs[-1]
    copies = [
        pltpu.make_async_copy(refs[i], refs[count + i], sems.at[i]) for i in range(count)
    ]
    for c in copies:
        c.start()
    for c in copies:
        c.wait()


def body(dims, hyena_q, hyena_k, hyena_v, filters, norm_gain, attn_q, attn_k, out_grad, doc_lengths):
    contexts, mirrors, tensors = dims
    count = contexts * mirrors
    rows, channels = hyena_q.shape
    groups, taps = filters.shape
    heads = channels // HEAD
    share = groups // count
    slots = FIXED + tensors - 1 + 2 * (count - 1)
    window = (3 * rows, channels)
    tile = jax.ShapeDtypeStruct((rows, channels), BF16)
    vmem = pl.BlockSpec(memory_space=pltpu.VMEM)
    results = pl.pallas_call(
        functools.partial(kernel, dims),
        out_shape=(tile,) * 6 + (jax.ShapeDtypeStruct((groups, taps), F32),),
        in_specs=[vmem] * 8 + [pl.BlockSpec(memory_space=pltpu.SMEM)],
        out_specs=(vmem,) * 7,
        scratch_shapes=[
            pltpu.VMEM((groups, taps), F32),
            pltpu.VMEM((groups, taps), F32),
            pltpu.VMEM((taps + rows, channels), BF16),
            pltpu.VMEM((taps + rows, channels), BF16),
            pltpu.VMEM(window, BF16),
            pltpu.VMEM(window, BF16),
            pltpu.VMEM(window, BF16),
            pltpu.VMEM(window, BF16),
            pltpu.VMEM((3, heads, rows), F32),
            pltpu.VMEM((3, heads, rows), F32),
            pltpu.VMEM((heads, rows, 3 * rows), F32),
            pltpu.VMEM((heads, rows, 3 * rows), F32),
            pltpu.VMEM((rows, 3 * rows), F32),
            pltpu.VMEM((rows, 3 * rows), F32),
            pltpu.VMEM((rows, 2 * taps), BF16),
            pltpu.VMEM((rows, 2 * taps), BF16),
            pltpu.VMEM((rows, 2 * taps), F32),
            pltpu.VMEM((rows, channels), F32),
            pltpu.VMEM((rows, channels), F32),
            pltpu.VMEM((rows, LANES), F32),
            pltpu.VMEM((8, rows), F32),
            pltpu.VMEM((tensors - 1, 8, rows), F32),
            pltpu.VMEM((groups, taps), F32),
            pltpu.VMEM((count, share, taps), F32),
            pltpu.VMEM((count - 1, share, taps), F32),
            pltpu.VMEM((count, share, taps), F32),
            pltpu.SemaphoreType.DMA((slots,)),
            pltpu.SemaphoreType.DMA((slots,)),
        ],
        compiler_params=pltpu.CompilerParams(
            collective_id=0, has_side_effects=True, vmem_limit_bytes=(32 if rows <= 128 else 63) * 1024 * 1024
        ),
        name="hyena_attention",
    )(
        hyena_q, hyena_k, hyena_v, filters, norm_gain[None, :], attn_q, attn_k, out_grad,
        doc_lengths,
    )
    hbm = pl.BlockSpec(memory_space=pl.ANY)
    shapes = [jax.ShapeDtypeStruct(r.shape, r.dtype) for r in results]
    return pl.pallas_call(
        hand_on,
        out_shape=tuple(shapes),
        in_specs=[hbm] * len(shapes),
        out_specs=(hbm,) * len(shapes),
        scratch_shapes=[pltpu.SemaphoreType.DMA((len(shapes),))],
        name="hand_on",
    )(*results)


def solution(mesh):
    dims = (mesh.shape["context"], mesh.shape["mirror"], mesh.shape["tensor"])
    tokens = P(("context", "mirror"), "tensor")
    return jax.shard_map(
        functools.partial(body, dims),
        mesh=mesh,
        in_specs=(tokens, tokens, tokens, P("tensor", None), P("tensor"), tokens, tokens, tokens, P()),
        out_specs=(tokens,) * 6 + (P("tensor", None),),
        check_vma=False,
    )
```

```python
import functools

import jax
import jax.numpy as jnp
from jax import lax
from jax.experimental import pallas as pl
from jax.experimental.pallas import tpu as pltpu
from jax.sharding import PartitionSpec as P

HEAD = 128
LANES = 128
D = 8192
REACH = 2
NEG = -1e30
MESH = pl.DeviceIdType.MESH
F32 = jnp.float32
BF16 = jnp.bfloat16

CHUNKS = 2
VMEM_MOST = 63 * 1024 * 1024
KV, K2, K1, Q2, Q1, D2, D1, L1, L2, V2, V1, E1, E2, GS = range(14)
FIXED = 14 * CHUNKS


def dot_nt(a, b):
    return lax.dot_general(a, b, (((1,), (1,)), ((), ())), preferred_element_type=F32)


def dot_nn(a, b):
    return lax.dot_general(a, b, (((1,), (0,)), ((), ())), preferred_element_type=F32)


def kernel(
    dims,
    hq_hbm, hk_hbm, hv_hbm, filt_in, gain, aq_hbm, ak_hbm, og_hbm, lens,
    out_hbm, gq_hbm, gk_hbm, ghq_hbm, ghk_hbm, ghv_hbm, gfilt,
    hq, hk, hv, out, gq, gk, ghq, ghk, ghv, bands_back, filt, filt_rev, kvwin, gswin, kwin, vwin, qwin, dwin, lrow, erow, prob, prob_t,
    qbias, kbias, fmask, bmask, rmask, signal, gval, cols, stat_out, stat_in,
    gflat, gpart, gin, gsum, send, recv, load, store,
):
    contexts, mirrors, tensors = dims
    count = contexts * mirrors
    rows, channels = hq_hbm.shape
    groups, taps = filt_in.shape
    width = channels // groups
    per = LANES // width
    blocks = channels // LANES
    heads = channels // HEAD
    subs = rows // taps
    scale = HEAD ** (-0.5)
    ctx = lax.axis_index("context")
    mir = lax.axis_index("mirror")
    ten = lax.axis_index("tensor")
    me = ctx * mirrors + mir
    base = me * rows

    def token(index):
        index = lax.rem(index + 2 * count, count)
        return {"context": index // mirrors, "mirror": lax.rem(index, mirrors)}

    def peer(index):
        return {"tensor": lax.rem(index, tensors)}

    far, mid, near = pl.ds(0, rows), pl.ds(rows, rows), pl.ds(2 * rows, rows)
    loads = [
        pltpu.make_async_copy(src, dst, load.at[i])
        for i, (src, dst) in enumerate(
            [
                (ak_hbm, kwin.at[near]), (aq_hbm, qwin.at[far]), (og_hbm, dwin.at[far]),
                (hk_hbm, hk), (hv_hbm, hv), (hq_hbm, hq),
            ]
        )
    ]
    for c in loads:
        c.start()
    stores = [
        pltpu.make_async_copy(src, dst, store.at[i])
        for i, (src, dst) in enumerate(
            [
                (out, out_hbm), (gq, gq_hbm), (gk, gk_hbm), (ghq, ghq_hbm), (ghk, ghk_hbm),
                (ghv, ghv_hbm),
            ]
        )
    ]

    barrier = pltpu.get_barrier_semaphore()
    for d in range(1, count):
        pl.semaphore_signal(barrier, inc=1, device_id=token(me + d), device_id_type=MESH)
    for d in range(1, tensors):
        pl.semaphore_signal(barrier, inc=1, device_id=peer(ten + d), device_id_type=MESH)
    pl.semaphore_wait(barrier, count - 1 + tensors - 1)

    def copy(slot, src, dst, device):
        return pltpu.make_async_remote_copy(
            src_ref=src, dst_ref=dst, send_sem=send.at[slot], recv_sem=recv.at[slot],
            device_id=device, device_id_type=MESH,
        )

    first, last = ctx == 0, ctx == contexts - 1
    inner_lo, inner_hi = jnp.logical_not(first), jnp.logical_not(last)
    core0, core1 = mir == 0, mir == 1
    partner = token(me + 1 - 2 * mir)

    span = channels // CHUNKS
    own_tail = pl.ds(rows, taps)
    has_lo, has_hi = me > 0, me < count - 1

    def cut(c):
        return pl.ds(c * span, span)

    def chunked(slot, src, src_rows, dst, dst_rows, device):
        return [
            copy(slot * CHUNKS + c, src.at[src_rows, cut(c)], dst.at[dst_rows, cut(c)], device)
            for c in range(CHUNKS)
        ]

    c_kv = chunked(KV, kvwin, own_tail, kvwin, pl.ds(0, taps), token(me + 1))
    c_gs = chunked(GS, gswin, pl.ds(0, taps), gswin, pl.ds(rows, taps), token(me - 1))

    def forward(slot2, slot1, win):
        return (
            chunked(slot2, win, near, win, far, token(me + 2)),
            chunked(slot1, win, near, win, mid, partner),
            chunked(slot1, win, far, win, mid, partner),
        )

    def backward(slot2, slot1, win):
        return (
            chunked(slot2, win, far, win, near, token(me - 2)),
            chunked(slot1, win, far, win, mid, partner),
            chunked(slot1, win, near, win, mid, partner),
        )

    k_cp = forward(K2, K1, kwin)
    v_cp = forward(V2, V1, vwin)
    q_cp = backward(Q2, Q1, qwin)
    d_cp = backward(D2, D1, dwin)
    few = heads // CHUNKS

    def rows_back(slot1, slot2, ref):
        def one(slot, to, c, device):
            at = pl.ds(c * few, few)
            return copy(slot * CHUNKS + c, ref.at[0, at], ref.at[to, at], device)

        return (
            [one(slot1, 1, c, token(me - 1)) for c in range(CHUNKS)],
            [one(slot2, 2, c, token(me - 2)) for c in range(CHUNKS)],
        )

    l_cp = rows_back(L1, L2, lrow)
    e_cp = rows_back(E1, E2, erow)

    def when(cond, fn):
        pl.when(cond)(fn)

    def start_forward(cps, c):
        when(inner_hi, cps[0][c].start)
        when(core0, cps[1][c].start)

    def start_backward(cps, c):
        when(inner_lo, cps[0][c].start)
        when(core1, cps[1][c].start)

    def land_forward(cps, c):
        when(inner_lo, cps[0][c].wait_recv)
        when(jnp.logical_and(core1, inner_lo), cps[2][c].start)

    def land_backward(cps, c):
        when(inner_hi, cps[0][c].wait_recv)
        when(jnp.logical_and(core0, inner_hi), cps[2][c].start)

    def finish_forward(cps, c):
        when(jnp.logical_or(core1, inner_lo), cps[1][c].wait_recv)

    def finish_backward(cps, c):
        when(jnp.logical_or(core0, inner_hi), cps[1][c].wait_recv)

    def start_rows(cps, c):
        when(me > 0, cps[0][c].start)
        when(me > 1, cps[1][c].start)

    def finish_rows(cps, c):
        when(me < count - 1, cps[0][c].wait_recv)
        when(me < count - 2, cps[1][c].wait_recv)

    def drain_forward(cps, c):
        when(inner_hi, cps[0][c].wait_send)
        when(core0, cps[1][c].wait_send)
        when(jnp.logical_and(core1, inner_lo), cps[2][c].wait_send)

    def drain_backward(cps, c):
        when(inner_lo, cps[0][c].wait_send)
        when(core1, cps[1][c].wait_send)
        when(jnp.logical_and(core0, inner_hi), cps[2][c].wait_send)

    loads[0].wait()
    start_forward(k_cp, 0)
    loads[1].wait()
    start_backward(q_cp, 0)
    loads[2].wait()
    start_backward(d_cp, 0)
    loads[3].wait()
    loads[4].wait()
    kvwin[pl.ds(taps, rows)] = (hk[...].astype(F32) * hv[...].astype(F32)).astype(BF16)
    for c in range(CHUNKS):
        when(has_hi, c_kv[c].start)

    def zero(ref, at):
        ref[at] = jnp.zeros((ref[at].shape), ref.dtype)

    when(me == 0, lambda: zero(kvwin, pl.ds(0, taps)))
    when(me == count - 1, lambda: zero(gswin, pl.ds(rows, taps)))
    when(first, lambda: zero(kwin, far))
    when(first, lambda: zero(vwin, far))
    when(me == 0, lambda: zero(kwin, mid))
    when(me == 0, lambda: zero(vwin, mid))
    when(last, lambda: zero(qwin, near))
    when(last, lambda: zero(dwin, near))
    when(me == count - 1, lambda: zero(qwin, mid))
    when(me == count - 1, lambda: zero(dwin, mid))
    when(me == count - 1, lambda: zero(lrow, 1))
    when(me == count - 1, lambda: zero(erow, 1))
    when(me >= count - 2, lambda: zero(lrow, 2))
    when(me >= count - 2, lambda: zero(erow, 2))

    row_at = lax.broadcasted_iota(jnp.int32, (taps, taps), 0)
    col_at = lax.broadcasted_iota(jnp.int32, (taps, taps), 1)
    turn = jnp.where(lax.rem(row_at + col_at, taps) == 0, 1.0, 0.0).astype(BF16)
    filt[...] = filt_in[...].astype(F32)
    filt_rev[...] = dot_nn(filt_in[...], turn)

    ends = []
    total = jnp.int32(0)
    for i in range(lens.shape[0]):
        total = total + lens[i]
        ends.append(total)

    def doc(pos):
        return sum((pos >= e).astype(jnp.int32) for e in ends)

    def grid(shape, row0, col0):
        return (
            row0 + lax.broadcasted_iota(jnp.int32, shape, 0),
            col0 + lax.broadcasted_iota(jnp.int32, shape, 1),
        )

    t_pos, u_pos = grid((rows, 3 * rows), base, base - 2 * rows)
    ok = (u_pos >= 0) & (u_pos <= t_pos) & (t_pos - u_pos <= REACH * rows) & (doc(u_pos) == doc(t_pos))
    qbias[...] = jnp.where(ok, 0.0, NEG)
    u_pos, t_pos = grid((rows, 3 * rows), base, base)
    ok = (u_pos <= t_pos) & (t_pos - u_pos <= REACH * rows) & (doc(u_pos) == doc(t_pos))
    kbias[...] = jnp.where(ok, 0.0, NEG)
    for s in range(subs):
        at = pl.ds(s * taps, taps)
        t_pos, u_pos = grid((taps, 2 * taps), base + s * taps, base + (s - 1) * taps)
        ok = (u_pos >= 0) & (u_pos <= t_pos) & (t_pos - u_pos < taps) & (doc(u_pos) == doc(t_pos))
        fmask[at] = jnp.where(ok, 1.0, 0.0).astype(BF16)
        halves = []
        for i in range(2):
            t_pos, w_pos = grid((taps, taps), base + s * taps, 0)
            u_pos = base + (s - 1 + i) * taps + lax.rem(taps - w_pos, taps)
            ok = (u_pos >= 0) & (u_pos <= t_pos) & (t_pos - u_pos < taps) & (doc(u_pos) == doc(t_pos))
            halves.append(jnp.where(ok, 1.0, 0.0))
        rmask[at] = jnp.concatenate(halves, axis=1)
        t_pos, u_pos = grid((taps, 2 * taps), base + s * taps, base + s * taps)
        ok = (u_pos >= t_pos) & (u_pos - t_pos < taps) & (doc(u_pos) == doc(t_pos))
        bmask[at] = jnp.where(ok, 1.0, 0.0).astype(BF16)

    lane = lax.broadcasted_iota(jnp.int32, (taps, LANES), 1)

    def chan(b):
        return pl.ds(pl.multiple_of(b * LANES, LANES), LANES)

    def toeplitz(ref, b):
        made = []
        for i in range(per):
            row = jnp.broadcast_to(ref[pl.ds(b * per + i, 1), :], (taps, taps))
            made.append(pltpu.roll(row, 0, 1, stride=1, stride_axis=0).astype(BF16))
        return made

    def stacked(bands, mask):
        mask_lo, mask_hi = mask[:, :taps], mask[:, taps:]
        return jnp.concatenate(
            [jnp.concatenate([band * mask_lo, band * mask_hi], axis=1) for band in bands], axis=0
        )

    def conv(stack, window):
        every = dot_nn(stack, window)
        picked = every[:taps]
        for i in range(1, per):
            picked = jnp.where(lane >= i * width, every[i * taps : (i + 1) * taps], picked)
        return picked

    early = bands_back.shape[0] == blocks

    def band_step(b, carry):
        bands_back[b] = stacked(toeplitz(filt, b), bmask[...])
        return carry

    if early:
        lax.fori_loop(0, blocks, band_step, 0, unroll=2)

    start_forward(k_cp, 1)
    start_backward(q_cp, 1)
    loads[5].wait()

    def signal_step(b, acc):
        at = chan(b)
        bands = toeplitz(filt_rev, b)
        parts = []
        for s in range(subs):
            here = pl.ds(s * taps, taps)
            made = conv(stacked(bands, fmask[here]), kvwin[pl.ds(s * taps, 2 * taps), at])
            signal[here, at] = made
            mix = hq[here, at].astype(F32) * made
            parts.append(mix * mix)
        return acc + jnp.concatenate(parts, axis=0)

    col_lane = lax.broadcasted_iota(jnp.int32, (rows, LANES), 1)

    def lse_step(h, acc):
        at = chan(h)
        score = dot_nt(qwin[far, at], kwin[:, at]) * scale + qbias[...]
        top = jnp.max(score, axis=1, keepdims=True)
        raised = jnp.exp(score - top)
        total = jnp.sum(raised, axis=1, keepdims=True)
        lse = top + jnp.log(total)
        prob[h] = raised * (1.0 / total)
        return jnp.where(col_lane == h, lse, acc)

    zeros = jnp.zeros((rows, LANES), F32)

    def over_heads(step, c, acc, unroll=4):
        return lax.fori_loop(c * few, (c + 1) * few, step, acc, unroll=unroll)

    for c in range(CHUNKS):
        land_forward(k_cp, c)
        finish_forward(k_cp, c)
        cols[...] = over_heads(lse_step, c, zeros)
        lrow[0, c * few : (c + 1) * few] = jnp.transpose(cols[...])[c * few : (c + 1) * few]
        start_rows(l_cp, c)
        if c == 0:
            start_backward(d_cp, 1)

    def wide_row(ref, h):
        return jnp.concatenate([ref[j, pl.ds(h, 1), :] for j in range(3)], axis=1)

    def gval_step(h, acc):
        at = chan(h)
        score = dot_nt(kwin[near, at], qwin[:, at]) * scale + kbias[...]
        p = jnp.exp(score - wide_row(lrow, h))
        prob_t[h] = p
        made = dot_nn(p.astype(BF16), dwin[:, at])
        gval[:, at] = made
        return acc + gain[:, at] * made * (hq[:, at].astype(F32) * signal[:, at])

    squares = inner = zeros
    for c in range(CHUNKS):
        when(has_lo, c_kv[c].wait_recv)
        land_backward(q_cp, c)
        land_backward(d_cp, c)
        squares = over_heads(signal_step, c, squares, 2)
        finish_backward(q_cp, c)
        finish_backward(d_cp, c)
        finish_rows(l_cp, c)
        inner = over_heads(gval_step, c, inner)

    cols[...] = jnp.where(
        col_lane == 0,
        jnp.sum(squares, axis=1, keepdims=True),
        jnp.where(col_lane == 1, jnp.sum(inner, axis=1, keepdims=True), 0.0),
    )
    stat_out[...] = jnp.transpose(cols[...])[:8]
    stat_cp = [
        copy(FIXED + d - 1, stat_out, stat_in.at[d - 1], peer(ten + d)) for d in range(1, tensors)
    ]
    for c in stat_cp:
        c.start()
    for c in stat_cp:
        c.wait_recv()
    stats = stat_out[...]
    for d in range(1, tensors):
        stats = stats + stat_in[d - 1]
    stats = jnp.transpose(jnp.concatenate([stats, jnp.zeros((LANES - 8, rows), F32)], axis=0))
    inv = lax.rsqrt(stats[:, 0:1] / D + 1e-06)
    pull = stats[:, 1:2] * inv * inv / D

    def norm_step(b, carry):
        at = chan(b)
        gate = hq[:, at].astype(F32)
        made = signal[:, at]
        mix = gate * made
        gains = gain[:, at]
        vwin[near, at] = (mix * inv * gains).astype(BF16)
        grad_mix = inv * (gains * gval[:, at] - mix * pull)
        ghq[:, at] = (grad_mix * made).astype(BF16)
        gswin[pl.ds(0, rows), at] = (grad_mix * gate).astype(BF16)
        return carry

    for c in range(CHUNKS):
        over_heads(norm_step, c, 0)
        start_forward(v_cp, c)
        when(has_lo, c_gs[c].start)

    stores[3].start()

    def filter_step(b, carry):
        at = chan(b)
        sums = [jnp.zeros((1, taps), F32) for _ in range(per)]
        for s in range(subs):
            grads = gswin[pl.ds(s * taps, taps), at]
            stack = jnp.concatenate(
                [
                    jnp.where((lane >= i * width) & (lane < (i + 1) * width), grads, jnp.zeros_like(grads))
                    for i in range(per)
                ],
                axis=0,
            )
            turned = jnp.concatenate(
                [
                    dot_nn(turn, kvwin[pl.ds((s + i) * taps, taps), at]).astype(BF16)
                    for i in range(2)
                ],
                axis=0,
            )
            every = dot_nt(stack, turned)
            mask = rmask[pl.ds(s * taps, taps)]
            for i in range(per):
                part = every[i * taps : (i + 1) * taps] * mask
                part = part[:, :taps] + part[:, taps:]
                part = pltpu.roll(part, 0, 1, stride=1, stride_axis=0)
                sums[i] = sums[i] + jnp.sum(part, axis=0, keepdims=True)
        gflat[pl.ds(pl.multiple_of(b * per, per), per), :] = jnp.concatenate(sums, axis=0)
        return carry

    lax.fori_loop(0, blocks, filter_step, 0, unroll=2)
    share = groups // count
    for i in range(count):
        gpart[i] = gflat[i * share : (i + 1) * share]
    at0 = FIXED + tensors - 1
    scatter = [
        copy(at0 + d - 1, gpart.at[lax.rem(me + d, count)], gin.at[d - 1], token(me + d))
        for d in range(1, count)
    ]
    for c in scatter:
        c.start()

    def back_step(b, carry):
        at = chan(b)
        bands = None if early else toeplitz(filt, b)
        for s in range(subs):
            here = pl.ds(s * taps, taps)
            stack = bands_back[b] if early else stacked(bands, bmask[here])
            made = conv(stack, gswin[pl.ds(s * taps, 2 * taps), at])
            ghk[here, at] = (made * hv[here, at].astype(F32)).astype(BF16)
            ghv[here, at] = (made * hk[here, at].astype(F32)).astype(BF16)
        return carry

    at1 = at0 + count - 1
    gather = [
        copy(at1 + d - 1, gsum.at[me], gsum.at[me], token(me + d)) for d in range(1, count)
    ]

    def query_step(h, acc):
        at = chan(h)
        values = vwin[:, at]
        p = prob[h]
        grad_p = dot_nt(dwin[far, at], values)
        out[:, at] = dot_nn(p.astype(BF16), values).astype(BF16)
        delta = jnp.sum(p * grad_p, axis=1, keepdims=True)
        ds = (p * (grad_p - delta) * scale).astype(BF16)
        gq[:, at] = dot_nn(ds, kwin[:, at]).astype(BF16)
        return jnp.where(col_lane == h, delta, acc)

    for c in range(CHUNKS):
        when(has_hi, c_gs[c].wait_recv)
        land_forward(v_cp, c)
        over_heads(back_step, c, 0, 2)
        if c == CHUNKS - 1:
            stores[4].start()
            stores[5].start()
        if c == CHUNKS - 1:
            for d in scatter:
                d.wait_recv()
            mine = gpart[me]
            for d in range(1, count):
                mine = mine + gin[d - 1]
            gsum[me] = mine
            for d in gather:
                d.start()
        finish_forward(v_cp, c)
        cols[...] = over_heads(query_step, c, zeros)
        erow[0, c * few : (c + 1) * few] = jnp.transpose(cols[...])[c * few : (c + 1) * few]
        start_rows(e_cp, c)
        if c == CHUNKS - 1:
            stores[0].start()
            stores[1].start()

    for d in range(1, count):
        other = lax.rem(me - d + count, count)
        copy(at1 + d - 1, gsum.at[other], gsum.at[other], token(me + d)).wait_recv()
    for i in range(count):
        gfilt[i * share : (i + 1) * share] = gsum[i]

    def key_step(h, carry):
        at = chan(h)
        grad_p = dot_nt(vwin[near, at], dwin[:, at])
        ds = (prob_t[h] * (grad_p - wide_row(erow, h)) * scale).astype(BF16)
        gk[:, at] = dot_nn(ds, qwin[:, at]).astype(BF16)
        return carry

    for c in range(CHUNKS):
        finish_rows(e_cp, c)
        over_heads(key_step, c, 0)
    stores[2].start()

    for c in range(CHUNKS):
        when(has_hi, c_kv[c].wait_send)
        when(has_lo, c_gs[c].wait_send)
        drain_forward(k_cp, c)
        drain_forward(v_cp, c)
        drain_backward(q_cp, c)
        drain_backward(d_cp, c)
        for cps in (l_cp, e_cp):
            when(me > 0, cps[0][c].wait_send)
            when(me > 1, cps[1][c].wait_send)
    for c in stat_cp + scatter + gather:
        c.wait_send()
    for c in stores:
        c.wait()


def hand_on(*refs):
    count = (len(refs) - 2) // 3
    sources, results, held = refs[:count], refs[count : 2 * count], refs[2 * count : 3 * count]
    came, went = refs[-2:]
    loads = [pltpu.make_async_copy(sources[i], held[i], came.at[i]) for i in range(count)]
    stores = [pltpu.make_async_copy(held[i], results[i], went.at[i]) for i in range(count)]
    for c in loads:
        c.start()
    for first, then in zip(loads, stores):
        first.wait()
        then.start()
    for c in stores:
        c.wait()


def body(dims, hyena_q, hyena_k, hyena_v, filters, norm_gain, attn_q, attn_k, out_grad, doc_lengths):
    contexts, mirrors, tensors = dims
    count = contexts * mirrors
    rows, channels = hyena_q.shape
    groups, taps = filters.shape
    heads = channels // HEAD
    share = groups // count
    slots = FIXED + tensors - 1 + 2 * (count - 1)
    window = (3 * rows, channels)
    tile = jax.ShapeDtypeStruct((rows, channels), BF16)
    vmem = pl.BlockSpec(memory_space=pltpu.VMEM)
    hbm = pl.BlockSpec(memory_space=pl.ANY)
    blocks = channels // LANES
    band_shape = (blocks, groups // blocks * taps, 2 * taps) if rows == taps else (1, 8, LANES)
    results = pl.pallas_call(
        functools.partial(kernel, dims),
        out_shape=(tile,) * 6 + (jax.ShapeDtypeStruct((groups, taps), F32),),
        in_specs=[hbm] * 3 + [vmem] * 2 + [hbm] * 3 + [pl.BlockSpec(memory_space=pltpu.SMEM)],
        out_specs=(hbm,) * 6 + (vmem,),
        scratch_shapes=[pltpu.VMEM((rows, channels), BF16)] * 9
        + [
            pltpu.VMEM(band_shape, BF16),
            pltpu.VMEM((groups, taps), F32),
            pltpu.VMEM((groups, taps), F32),
            pltpu.VMEM((taps + rows, channels), BF16),
            pltpu.VMEM((taps + rows, channels), BF16),
            pltpu.VMEM(window, BF16),
            pltpu.VMEM(window, BF16),
            pltpu.VMEM(window, BF16),
            pltpu.VMEM(window, BF16),
            pltpu.VMEM((3, heads, rows), F32),
            pltpu.VMEM((3, heads, rows), F32),
            pltpu.VMEM((heads, rows, 3 * rows), F32),
            pltpu.VMEM((heads, rows, 3 * rows), F32),
            pltpu.VMEM((rows, 3 * rows), F32),
            pltpu.VMEM((rows, 3 * rows), F32),
            pltpu.VMEM((rows, 2 * taps), BF16),
            pltpu.VMEM((rows, 2 * taps), BF16),
            pltpu.VMEM((rows, 2 * taps), F32),
            pltpu.VMEM((rows, channels), F32),
            pltpu.VMEM((rows, channels), F32),
            pltpu.VMEM((rows, LANES), F32),
            pltpu.VMEM((8, rows), F32),
            pltpu.VMEM((tensors - 1, 8, rows), F32),
            pltpu.VMEM((groups, taps), F32),
            pltpu.VMEM((count, share, taps), F32),
            pltpu.VMEM((count - 1, share, taps), F32),
            pltpu.VMEM((count, share, taps), F32),
            pltpu.SemaphoreType.DMA((slots,)),
            pltpu.SemaphoreType.DMA((slots,)),
            pltpu.SemaphoreType.DMA((6,)),
            pltpu.SemaphoreType.DMA((6,)),
        ],
        compiler_params=pltpu.CompilerParams(
            collective_id=0, has_side_effects=True, vmem_limit_bytes=VMEM_MOST
        ),
        name="hyena_attention",
    )(
        hyena_q, hyena_k, hyena_v, filters, norm_gain[None, :], attn_q, attn_k, out_grad,
        doc_lengths,
    )
    shapes = [jax.ShapeDtypeStruct(r.shape, r.dtype) for r in results]
    return pl.pallas_call(
        hand_on,
        out_shape=tuple(shapes),
        in_specs=[hbm] * len(shapes),
        out_specs=(hbm,) * len(shapes),
        scratch_shapes=[pltpu.VMEM(x.shape, x.dtype) for x in shapes]
        + [pltpu.SemaphoreType.DMA((len(shapes),))] * 2,
        compiler_params=pltpu.CompilerParams(vmem_limit_bytes=VMEM_MOST),
        name="hand_on",
    )(*results)


def solution(mesh):
    dims = (mesh.shape["context"], mesh.shape["mirror"], mesh.shape["tensor"])
    tokens = P(("context", "mirror"), "tensor")
    return jax.shard_map(
        functools.partial(body, dims),
        mesh=mesh,
        in_specs=(tokens, tokens, tokens, P("tensor", None), P("tensor"), tokens, tokens, tokens, P()),
        out_specs=(tokens,) * 6 + (P("tensor", None),),
        check_vma=False,
    )
```

```python
import functools

import jax
import jax.numpy as jnp
from jax import lax
from jax.experimental import pallas as pl
from jax.experimental.pallas import tpu as pltpu
from jax.sharding import PartitionSpec as P

HEAD = 128
LANES = 128
D = 8192
REACH = 2
NEG = -1e30
MESH = pl.DeviceIdType.MESH
F32 = jnp.float32
BF16 = jnp.bfloat16

CHUNKS = 2
VMEM_MOST = 63 * 1024 * 1024
KV, K2, K1, Q2, Q1, D2, D1, L1, L2, V2, V1, E1, E2, GS = range(14)
FIXED = 14 * CHUNKS


def dot_nt(a, b):
    return lax.dot_general(a, b, (((1,), (1,)), ((), ())), preferred_element_type=F32)


def dot_nn(a, b):
    return lax.dot_general(a, b, (((1,), (0,)), ((), ())), preferred_element_type=F32)


def kernel(
    dims,
    hq_hbm, hk_hbm, hv_hbm, filt_in, gain, aq_hbm, ak_hbm, og_hbm, lens,
    out_hbm, gq_hbm, gk_hbm, ghq_hbm, ghk_hbm, ghv_hbm, gfilt,
    hq, hk, hv, out, gq, gk, ghq, ghk, ghv, bands_back, filt, filt_rev, kvwin, gswin, kwin, vwin, qwin, dwin, lrow, erow, prob, prob_t,
    qbias, kbias, fmask, bmask, rmask, signal, gval, cols, stat_out, stat_in,
    gflat, gpart, gin, gsum, send, recv, load, store,
):
    contexts, mirrors, tensors = dims
    count = contexts * mirrors
    rows, channels = hq_hbm.shape
    groups, taps = filt_in.shape
    width = channels // groups
    per = LANES // width
    blocks = channels // LANES
    heads = channels // HEAD
    subs = rows // taps
    scale = HEAD ** (-0.5)
    ctx = lax.axis_index("context")
    mir = lax.axis_index("mirror")
    ten = lax.axis_index("tensor")
    me = ctx * mirrors + mir
    base = me * rows

    def token(index):
        index = lax.rem(index + 2 * count, count)
        return {"context": index // mirrors, "mirror": lax.rem(index, mirrors)}

    def peer(index):
        return {"tensor": lax.rem(index, tensors)}

    far, mid, near = pl.ds(0, rows), pl.ds(rows, rows), pl.ds(2 * rows, rows)
    loads = [
        pltpu.make_async_copy(src, dst, load.at[i])
        for i, (src, dst) in enumerate(
            [
                (aq_hbm, qwin.at[far]), (hk_hbm, hk), (hv_hbm, hv), (ak_hbm, kwin.at[near]),
                (og_hbm, dwin.at[far]), (hq_hbm, hq),
            ]
        )
    ]
    for c in loads:
        c.start()
    stores = [
        pltpu.make_async_copy(src, dst, store.at[i])
        for i, (src, dst) in enumerate(
            [
                (out, out_hbm), (gq, gq_hbm), (gk, gk_hbm), (ghq, ghq_hbm), (ghk, ghk_hbm),
                (ghv, ghv_hbm),
            ]
        )
    ]

    barrier = pltpu.get_barrier_semaphore()
    for d in range(1, count):
        pl.semaphore_signal(barrier, inc=1, device_id=token(me + d), device_id_type=MESH)
    for d in range(1, tensors):
        pl.semaphore_signal(barrier, inc=1, device_id=peer(ten + d), device_id_type=MESH)
    pl.semaphore_wait(barrier, count - 1 + tensors - 1)

    def copy(slot, src, dst, device):
        return pltpu.make_async_remote_copy(
            src_ref=src, dst_ref=dst, send_sem=send.at[slot], recv_sem=recv.at[slot],
            device_id=device, device_id_type=MESH,
        )

    first, last = ctx == 0, ctx == contexts - 1
    inner_lo, inner_hi = jnp.logical_not(first), jnp.logical_not(last)
    core0, core1 = mir == 0, mir == 1
    partner = token(me + 1 - 2 * mir)

    span = channels // CHUNKS
    own_tail = pl.ds(rows, taps)
    has_lo, has_hi = me > 0, me < count - 1

    def cut(c):
        return pl.ds(c * span, span)

    def chunked(slot, src, src_rows, dst, dst_rows, device):
        return [
            copy(slot * CHUNKS + c, src.at[src_rows, cut(c)], dst.at[dst_rows, cut(c)], device)
            for c in range(CHUNKS)
        ]

    c_kv = chunked(KV, kvwin, own_tail, kvwin, pl.ds(0, taps), token(me + 1))
    c_gs = chunked(GS, gswin, pl.ds(0, taps), gswin, pl.ds(rows, taps), token(me - 1))

    def forward(slot2, slot1, win):
        return (
            chunked(slot2, win, near, win, far, token(me + 2)),
            chunked(slot1, win, near, win, mid, partner),
            chunked(slot1, win, far, win, mid, partner),
        )

    def backward(slot2, slot1, win):
        return (
            chunked(slot2, win, far, win, near, token(me - 2)),
            chunked(slot1, win, far, win, mid, partner),
            chunked(slot1, win, near, win, mid, partner),
        )

    k_cp = forward(K2, K1, kwin)
    v_cp = forward(V2, V1, vwin)
    q_cp = backward(Q2, Q1, qwin)
    d_cp = backward(D2, D1, dwin)
    few = heads // CHUNKS

    def rows_back(slot1, slot2, ref):
        def one(slot, to, c, device):
            at = pl.ds(c * few, few)
            return copy(slot * CHUNKS + c, ref.at[0, at], ref.at[to, at], device)

        return (
            [one(slot1, 1, c, token(me - 1)) for c in range(CHUNKS)],
            [one(slot2, 2, c, token(me - 2)) for c in range(CHUNKS)],
        )

    l_cp = rows_back(L1, L2, lrow)
    e_cp = rows_back(E1, E2, erow)

    def when(cond, fn):
        pl.when(cond)(fn)

    def start_forward(cps, c):
        when(inner_hi, cps[0][c].start)
        when(core0, cps[1][c].start)

    def start_backward(cps, c):
        when(inner_lo, cps[0][c].start)
        when(core1, cps[1][c].start)

    def land_forward(cps, c):
        when(inner_lo, cps[0][c].wait_recv)
        when(jnp.logical_and(core1, inner_lo), cps[2][c].start)

    def land_backward(cps, c):
        when(inner_hi, cps[0][c].wait_recv)
        when(jnp.logical_and(core0, inner_hi), cps[2][c].start)

    def finish_forward(cps, c):
        when(jnp.logical_or(core1, inner_lo), cps[1][c].wait_recv)

    def finish_backward(cps, c):
        when(jnp.logical_or(core0, inner_hi), cps[1][c].wait_recv)

    def start_rows(cps, c):
        when(me > 0, cps[0][c].start)
        when(me > 1, cps[1][c].start)

    def finish_rows(cps, c):
        when(me < count - 1, cps[0][c].wait_recv)
        when(me < count - 2, cps[1][c].wait_recv)

    def drain_forward(cps, c):
        when(inner_hi, cps[0][c].wait_send)
        when(core0, cps[1][c].wait_send)
        when(jnp.logical_and(core1, inner_lo), cps[2][c].wait_send)

    def drain_backward(cps, c):
        when(inner_lo, cps[0][c].wait_send)
        when(core1, cps[1][c].wait_send)
        when(jnp.logical_and(core0, inner_hi), cps[2][c].wait_send)

    loads[0].wait()
    start_backward(q_cp, 0)
    loads[1].wait()
    loads[2].wait()
    kvwin[pl.ds(taps, rows)] = (hk[...].astype(F32) * hv[...].astype(F32)).astype(BF16)
    for c in range(CHUNKS):
        when(has_hi, c_kv[c].start)
    loads[3].wait()
    start_forward(k_cp, 0)
    loads[4].wait()
    start_backward(d_cp, 0)
    start_backward(q_cp, 1)
    start_forward(k_cp, 1)

    def zero(ref, at):
        ref[at] = jnp.zeros((ref[at].shape), ref.dtype)

    when(me == 0, lambda: zero(kvwin, pl.ds(0, taps)))
    when(me == count - 1, lambda: zero(gswin, pl.ds(rows, taps)))
    when(first, lambda: zero(kwin, far))
    when(first, lambda: zero(vwin, far))
    when(me == 0, lambda: zero(kwin, mid))
    when(me == 0, lambda: zero(vwin, mid))
    when(last, lambda: zero(qwin, near))
    when(last, lambda: zero(dwin, near))
    when(me == count - 1, lambda: zero(qwin, mid))
    when(me == count - 1, lambda: zero(dwin, mid))
    when(me == count - 1, lambda: zero(lrow, 1))
    when(me == count - 1, lambda: zero(erow, 1))
    when(me >= count - 2, lambda: zero(lrow, 2))
    when(me >= count - 2, lambda: zero(erow, 2))

    row_at = lax.broadcasted_iota(jnp.int32, (taps, taps), 0)
    col_at = lax.broadcasted_iota(jnp.int32, (taps, taps), 1)
    turn = jnp.where(lax.rem(row_at + col_at, taps) == 0, 1.0, 0.0).astype(BF16)
    filt[...] = filt_in[...].astype(F32)
    filt_rev[...] = dot_nn(filt_in[...], turn)

    ends = []
    total = jnp.int32(0)
    for i in range(lens.shape[0]):
        total = total + lens[i]
        ends.append(total)

    def doc(pos):
        return sum((pos >= e).astype(jnp.int32) for e in ends)

    def grid(shape, row0, col0):
        return (
            row0 + lax.broadcasted_iota(jnp.int32, shape, 0),
            col0 + lax.broadcasted_iota(jnp.int32, shape, 1),
        )

    t_pos, u_pos = grid((rows, 3 * rows), base, base - 2 * rows)
    ok = (u_pos >= 0) & (u_pos <= t_pos) & (t_pos - u_pos <= REACH * rows) & (doc(u_pos) == doc(t_pos))
    qbias[...] = jnp.where(ok, 0.0, NEG)
    u_pos, t_pos = grid((rows, 3 * rows), base, base)
    ok = (u_pos <= t_pos) & (t_pos - u_pos <= REACH * rows) & (doc(u_pos) == doc(t_pos))
    kbias[...] = jnp.where(ok, 0.0, NEG)
    for s in range(subs):
        at = pl.ds(s * taps, taps)
        t_pos, u_pos = grid((taps, 2 * taps), base + s * taps, base + (s - 1) * taps)
        ok = (u_pos >= 0) & (u_pos <= t_pos) & (t_pos - u_pos < taps) & (doc(u_pos) == doc(t_pos))
        fmask[at] = jnp.where(ok, 1.0, 0.0).astype(BF16)
        halves = []
        for i in range(2):
            t_pos, w_pos = grid((taps, taps), base + s * taps, 0)
            u_pos = base + (s - 1 + i) * taps + lax.rem(taps - w_pos, taps)
            ok = (u_pos >= 0) & (u_pos <= t_pos) & (t_pos - u_pos < taps) & (doc(u_pos) == doc(t_pos))
            halves.append(jnp.where(ok, 1.0, 0.0))
        rmask[at] = jnp.concatenate(halves, axis=1)
        t_pos, u_pos = grid((taps, 2 * taps), base + s * taps, base + s * taps)
        ok = (u_pos >= t_pos) & (u_pos - t_pos < taps) & (doc(u_pos) == doc(t_pos))
        bmask[at] = jnp.where(ok, 1.0, 0.0).astype(BF16)

    lane = lax.broadcasted_iota(jnp.int32, (taps, LANES), 1)

    def chan(b):
        return pl.ds(pl.multiple_of(b * LANES, LANES), LANES)

    def toeplitz(ref, b):
        made = []
        for i in range(per):
            row = jnp.broadcast_to(ref[pl.ds(b * per + i, 1), :], (taps, taps))
            made.append(pltpu.roll(row, 0, 1, stride=1, stride_axis=0).astype(BF16))
        return made

    def stacked(bands, mask):
        mask_lo, mask_hi = mask[:, :taps], mask[:, taps:]
        return jnp.concatenate(
            [jnp.concatenate([band * mask_lo, band * mask_hi], axis=1) for band in bands], axis=0
        )

    def conv(stack, window):
        every = dot_nn(stack, window)
        picked = every[:taps]
        for i in range(1, per):
            picked = jnp.where(lane >= i * width, every[i * taps : (i + 1) * taps], picked)
        return picked

    early = bands_back.shape[0] == blocks

    def band_step(b, carry):
        bands_back[b] = stacked(toeplitz(filt, b), bmask[...])
        return carry

    if early:
        lax.fori_loop(0, blocks, band_step, 0, unroll=2)

    start_backward(d_cp, 1)
    loads[5].wait()

    def signal_step(b, acc):
        at = chan(b)
        bands = toeplitz(filt_rev, b)
        parts = []
        for s in range(subs):
            here = pl.ds(s * taps, taps)
            made = conv(stacked(bands, fmask[here]), kvwin[pl.ds(s * taps, 2 * taps), at])
            signal[here, at] = made
            mix = hq[here, at].astype(F32) * made
            parts.append(mix * mix)
        return acc + jnp.concatenate(parts, axis=0)

    col_lane = lax.broadcasted_iota(jnp.int32, (rows, LANES), 1)

    def lse_step(h, acc):
        at = chan(h)
        score = dot_nt(qwin[far, at], kwin[:, at]) * scale + qbias[...]
        top = jnp.max(score, axis=1, keepdims=True)
        raised = jnp.exp(score - top)
        total = jnp.sum(raised, axis=1, keepdims=True)
        lse = top + jnp.log(total)
        prob[h] = raised * (1.0 / total)
        return jnp.where(col_lane == h, lse, acc)

    zeros = jnp.zeros((rows, LANES), F32)

    def over_heads(step, c, acc, unroll=4):
        return lax.fori_loop(c * few, (c + 1) * few, step, acc, unroll=unroll)

    def wide_row(ref, h):
        return jnp.concatenate([ref[j, pl.ds(h, 1), :] for j in range(3)], axis=1)

    def gval_step(h, acc):
        at = chan(h)
        score = dot_nt(kwin[near, at], qwin[:, at]) * scale + kbias[...]
        p = jnp.exp(score - wide_row(lrow, h))
        prob_t[h] = p
        made = dot_nn(p.astype(BF16), dwin[:, at])
        gval[:, at] = made
        return acc + gain[:, at] * made * (hq[:, at].astype(F32) * signal[:, at])

    def exchange(which, partial):
        total = jnp.sum(partial, axis=1, keepdims=True)
        cols[...] = jnp.where(col_lane == 0, total, 0.0)
        stat_out[which] = jnp.transpose(cols[...])[:8]
        cps = [
            copy(
                FIXED + which * (tensors - 1) + d - 1,
                stat_out.at[which], stat_in.at[which, d - 1], peer(ten + d),
            )
            for d in range(1, tensors)
        ]
        for c in cps:
            c.start()
        return cps

    def exchanged(which, cps):
        for c in cps:
            c.wait_recv()
        stats = stat_out[which]
        for d in range(1, tensors):
            stats = stats + stat_in[which, d - 1]
        stats = jnp.concatenate([stats, jnp.zeros((LANES - 8, rows), F32)], axis=0)
        return jnp.transpose(stats)[:, 0:1]

    def lse_chunk(c):
        land_forward(k_cp, c)
        finish_forward(k_cp, c)
        cols[...] = over_heads(lse_step, c, zeros)
        lrow[0, c * few : (c + 1) * few] = jnp.transpose(cols[...])[c * few : (c + 1) * few]
        start_rows(l_cp, c)

    squares = inner = zeros
    for c in range(CHUNKS):
        when(has_lo, c_kv[c].wait_recv)
        squares = over_heads(signal_step, c, squares, 2)
    square_cp = exchange(0, squares)
    lse_chunk(0)
    inv = lax.rsqrt(exchanged(0, square_cp) / D + 1e-06)

    def value_step(b, carry):
        at = chan(b)
        mix = hq[:, at].astype(F32) * signal[:, at]
        vwin[near, at] = (mix * inv * gain[:, at]).astype(BF16)
        return carry

    for c in range(CHUNKS):
        over_heads(value_step, c, 0)
        start_forward(v_cp, c)
    for c in range(1, CHUNKS):
        lse_chunk(c)

    for c in range(CHUNKS):
        land_backward(q_cp, c)
        land_backward(d_cp, c)
        finish_backward(q_cp, c)
        finish_backward(d_cp, c)
        finish_rows(l_cp, c)
        inner = over_heads(gval_step, c, inner)
    inner_cp = exchange(1, inner)

    def query_step(h, acc):
        at = chan(h)
        values = vwin[:, at]
        p = prob[h]
        grad_p = dot_nt(dwin[far, at], values)
        out[:, at] = dot_nn(p.astype(BF16), values).astype(BF16)
        delta = jnp.sum(p * grad_p, axis=1, keepdims=True)
        ds = (p * (grad_p - delta) * scale).astype(BF16)
        gq[:, at] = dot_nn(ds, kwin[:, at]).astype(BF16)
        return jnp.where(col_lane == h, delta, acc)

    def query_chunk(c):
        land_forward(v_cp, c)
        finish_forward(v_cp, c)
        cols[...] = over_heads(query_step, c, zeros)
        erow[0, c * few : (c + 1) * few] = jnp.transpose(cols[...])[c * few : (c + 1) * few]
        start_rows(e_cp, c)
    query_chunk(0)
    pull = exchanged(1, inner_cp) * inv * inv / D

    def norm_step(b, carry):
        at = chan(b)
        gate = hq[:, at].astype(F32)
        made = signal[:, at]
        grad_mix = inv * (gain[:, at] * gval[:, at] - gate * made * pull)
        ghq[:, at] = (grad_mix * made).astype(BF16)
        gswin[pl.ds(0, rows), at] = (grad_mix * gate).astype(BF16)
        return carry

    for c in range(CHUNKS):
        over_heads(norm_step, c, 0)
        when(has_lo, c_gs[c].start)
    stores[3].start()
    for c in range(1, CHUNKS):
        query_chunk(c)
    stores[0].start()
    stores[1].start()

    def filter_step(b, carry):
        at = chan(b)
        sums = [jnp.zeros((1, taps), F32) for _ in range(per)]
        for s in range(subs):
            grads = gswin[pl.ds(s * taps, taps), at]
            stack = jnp.concatenate(
                [
                    jnp.where((lane >= i * width) & (lane < (i + 1) * width), grads, jnp.zeros_like(grads))
                    for i in range(per)
                ],
                axis=0,
            )
            turned = jnp.concatenate(
                [
                    dot_nn(turn, kvwin[pl.ds((s + i) * taps, taps), at]).astype(BF16)
                    for i in range(2)
                ],
                axis=0,
            )
            every = dot_nt(stack, turned)
            mask = rmask[pl.ds(s * taps, taps)]
            for i in range(per):
                part = every[i * taps : (i + 1) * taps] * mask
                part = part[:, :taps] + part[:, taps:]
                part = pltpu.roll(part, 0, 1, stride=1, stride_axis=0)
                sums[i] = sums[i] + jnp.sum(part, axis=0, keepdims=True)
        gflat[pl.ds(pl.multiple_of(b * per, per), per), :] = jnp.concatenate(sums, axis=0)
        return carry

    lax.fori_loop(0, blocks, filter_step, 0, unroll=2)
    share = groups // count
    for i in range(count):
        gpart[i] = gflat[i * share : (i + 1) * share]
    at0 = FIXED + 2 * (tensors - 1)
    scatter = [
        copy(at0 + d - 1, gpart.at[lax.rem(me + d, count)], gin.at[d - 1], token(me + d))
        for d in range(1, count)
    ]
    for c in scatter:
        c.start()

    def back_step(b, carry):
        at = chan(b)
        bands = None if early else toeplitz(filt, b)
        for s in range(subs):
            here = pl.ds(s * taps, taps)
            stack = bands_back[b] if early else stacked(bands, bmask[here])
            made = conv(stack, gswin[pl.ds(s * taps, 2 * taps), at])
            ghk[here, at] = (made * hv[here, at].astype(F32)).astype(BF16)
            ghv[here, at] = (made * hk[here, at].astype(F32)).astype(BF16)
        return carry

    at1 = at0 + count - 1
    gather = [
        copy(at1 + d - 1, gsum.at[me], gsum.at[me], token(me + d)) for d in range(1, count)
    ]

    for c in range(CHUNKS):
        when(has_hi, c_gs[c].wait_recv)
        over_heads(back_step, c, 0, 2)
    stores[4].start()
    stores[5].start()
    for d in scatter:
        d.wait_recv()
    mine = gpart[me]
    for d in range(1, count):
        mine = mine + gin[d - 1]
    gsum[me] = mine
    for d in gather:
        d.start()

    def key_step(h, carry):
        at = chan(h)
        grad_p = dot_nt(vwin[near, at], dwin[:, at])
        ds = (prob_t[h] * (grad_p - wide_row(erow, h)) * scale).astype(BF16)
        gk[:, at] = dot_nn(ds, qwin[:, at]).astype(BF16)
        return carry

    for c in range(CHUNKS):
        finish_rows(e_cp, c)
        over_heads(key_step, c, 0)
    stores[2].start()

    for d in range(1, count):
        other = lax.rem(me - d + count, count)
        copy(at1 + d - 1, gsum.at[other], gsum.at[other], token(me + d)).wait_recv()
    for i in range(count):
        gfilt[i * share : (i + 1) * share] = gsum[i]

    for c in range(CHUNKS):
        when(has_hi, c_kv[c].wait_send)
        when(has_lo, c_gs[c].wait_send)
        drain_forward(k_cp, c)
        drain_forward(v_cp, c)
        drain_backward(q_cp, c)
        drain_backward(d_cp, c)
        for cps in (l_cp, e_cp):
            when(me > 0, cps[0][c].wait_send)
            when(me > 1, cps[1][c].wait_send)
    for c in square_cp + inner_cp + scatter + gather:
        c.wait_send()
    for c in stores:
        c.wait()


def hand_on(*refs):
    count = (len(refs) - 2) // 3
    sources, results, held = refs[:count], refs[count : 2 * count], refs[2 * count : 3 * count]
    came, went = refs[-2:]
    loads = [pltpu.make_async_copy(sources[i], held[i], came.at[i]) for i in range(count)]
    stores = [pltpu.make_async_copy(held[i], results[i], went.at[i]) for i in range(count)]
    for c in loads:
        c.start()
    for first, then in zip(loads, stores):
        first.wait()
        then.start()
    for c in stores:
        c.wait()


def body(dims, hyena_q, hyena_k, hyena_v, filters, norm_gain, attn_q, attn_k, out_grad, doc_lengths):
    contexts, mirrors, tensors = dims
    count = contexts * mirrors
    rows, channels = hyena_q.shape
    groups, taps = filters.shape
    heads = channels // HEAD
    share = groups // count
    slots = FIXED + 2 * (tensors - 1) + 2 * (count - 1)
    window = (3 * rows, channels)
    tile = jax.ShapeDtypeStruct((rows, channels), BF16)
    vmem = pl.BlockSpec(memory_space=pltpu.VMEM)
    hbm = pl.BlockSpec(memory_space=pl.ANY)
    blocks = channels // LANES
    band_shape = (blocks, groups // blocks * taps, 2 * taps) if rows == taps else (1, 8, LANES)
    results = pl.pallas_call(
        functools.partial(kernel, dims),
        out_shape=(tile,) * 6 + (jax.ShapeDtypeStruct((groups, taps), F32),),
        in_specs=[hbm] * 3 + [vmem] * 2 + [hbm] * 3 + [pl.BlockSpec(memory_space=pltpu.SMEM)],
        out_specs=(hbm,) * 6 + (vmem,),
        scratch_shapes=[pltpu.VMEM((rows, channels), BF16)] * 9
        + [
            pltpu.VMEM(band_shape, BF16),
            pltpu.VMEM((groups, taps), F32),
            pltpu.VMEM((groups, taps), F32),
            pltpu.VMEM((taps + rows, channels), BF16),
            pltpu.VMEM((taps + rows, channels), BF16),
            pltpu.VMEM(window, BF16),
            pltpu.VMEM(window, BF16),
            pltpu.VMEM(window, BF16),
            pltpu.VMEM(window, BF16),
            pltpu.VMEM((3, heads, rows), F32),
            pltpu.VMEM((3, heads, rows), F32),
            pltpu.VMEM((heads, rows, 3 * rows), F32),
            pltpu.VMEM((heads, rows, 3 * rows), F32),
            pltpu.VMEM((rows, 3 * rows), F32),
            pltpu.VMEM((rows, 3 * rows), F32),
            pltpu.VMEM((rows, 2 * taps), BF16),
            pltpu.VMEM((rows, 2 * taps), BF16),
            pltpu.VMEM((rows, 2 * taps), F32),
            pltpu.VMEM((rows, channels), F32),
            pltpu.VMEM((rows, channels), F32),
            pltpu.VMEM((rows, LANES), F32),
            pltpu.VMEM((2, 8, rows), F32),
            pltpu.VMEM((2, tensors - 1, 8, rows), F32),
            pltpu.VMEM((groups, taps), F32),
            pltpu.VMEM((count, share, taps), F32),
            pltpu.VMEM((count - 1, share, taps), F32),
            pltpu.VMEM((count, share, taps), F32),
            pltpu.SemaphoreType.DMA((slots,)),
            pltpu.SemaphoreType.DMA((slots,)),
            pltpu.SemaphoreType.DMA((6,)),
            pltpu.SemaphoreType.DMA((6,)),
        ],
        compiler_params=pltpu.CompilerParams(
            collective_id=0, has_side_effects=True, vmem_limit_bytes=VMEM_MOST
        ),
        name="hyena_attention",
    )(
        hyena_q, hyena_k, hyena_v, filters, norm_gain[None, :], attn_q, attn_k, out_grad,
        doc_lengths,
    )
    shapes = [jax.ShapeDtypeStruct(r.shape, r.dtype) for r in results]
    return pl.pallas_call(
        hand_on,
        out_shape=tuple(shapes),
        in_specs=[hbm] * len(shapes),
        out_specs=(hbm,) * len(shapes),
        scratch_shapes=[pltpu.VMEM(x.shape, x.dtype) for x in shapes]
        + [pltpu.SemaphoreType.DMA((len(shapes),))] * 2,
        compiler_params=pltpu.CompilerParams(vmem_limit_bytes=VMEM_MOST),
        name="hand_on",
    )(*results)


def solution(mesh):
    dims = (mesh.shape["context"], mesh.shape["mirror"], mesh.shape["tensor"])
    tokens = P(("context", "mirror"), "tensor")
    return jax.shard_map(
        functools.partial(body, dims),
        mesh=mesh,
        in_specs=(tokens, tokens, tokens, P("tensor", None), P("tensor"), tokens, tokens, tokens, P()),
        out_specs=(tokens,) * 6 + (P("tensor", None),),
        check_vma=False,
    )
```

```python
import functools

import jax
import jax.numpy as jnp
from jax import lax
from jax.experimental import pallas as pl
from jax.experimental.pallas import tpu as pltpu
from jax.sharding import PartitionSpec as P

HEAD = 128
LANES = 128
D = 8192
REACH = 2
NEG = -1e30
MESH = pl.DeviceIdType.MESH
F32 = jnp.float32
BF16 = jnp.bfloat16

CHUNKS = 2
VMEM_MOST = 63 * 1024 * 1024
KV, K2, K1, Q2, Q1, D2, D1, L1, L2, V2, V1, E1, E2, GS = range(14)
FIXED = 14 * CHUNKS


def dot_nt(a, b):
    return lax.dot_general(a, b, (((1,), (1,)), ((), ())), preferred_element_type=F32)


def dot_nn(a, b):
    return lax.dot_general(a, b, (((1,), (0,)), ((), ())), preferred_element_type=F32)


def kernel(
    dims,
    hq_hbm, hk_hbm, hv_hbm, filt_in, gain, aq_hbm, ak_hbm, og_hbm, lens,
    out_hbm, gq_hbm, gk_hbm, ghq_hbm, ghk_hbm, ghv_hbm, gfilt,
    hq, hk, hv, out, gq, gk, ghq, ghk, ghv, bands_back, filt, filt_rev, kvturn, kvwin, gswin, kwin, vwin, qwin, dwin, lrow, erow, prob, prob_t,
    qbias, kbias, fmask, bmask, rmask, signal, gval, cols, stat_out, stat_in,
    gflat, gpart, gin, gsum, send, recv, load, store,
):
    contexts, mirrors, tensors = dims
    count = contexts * mirrors
    rows, channels = hq_hbm.shape
    groups, taps = filt_in.shape
    width = channels // groups
    per = LANES // width
    blocks = channels // LANES
    heads = channels // HEAD
    subs = rows // taps
    scale = HEAD ** (-0.5)
    ctx = lax.axis_index("context")
    mir = lax.axis_index("mirror")
    ten = lax.axis_index("tensor")
    me = ctx * mirrors + mir
    base = me * rows

    def token(index):
        index = lax.rem(index + 2 * count, count)
        return {"context": index // mirrors, "mirror": lax.rem(index, mirrors)}

    def peer(index):
        return {"tensor": lax.rem(index, tensors)}

    far, mid, near = pl.ds(0, rows), pl.ds(rows, rows), pl.ds(2 * rows, rows)
    loads = [
        pltpu.make_async_copy(src, dst, load.at[i])
        for i, (src, dst) in enumerate(
            [
                (aq_hbm, qwin.at[far]), (hk_hbm, hk), (hv_hbm, hv), (ak_hbm, kwin.at[near]),
                (og_hbm, dwin.at[far]), (hq_hbm, hq),
            ]
        )
    ]
    for c in loads:
        c.start()
    stores = [
        pltpu.make_async_copy(src, dst, store.at[i])
        for i, (src, dst) in enumerate(
            [
                (out, out_hbm), (gq, gq_hbm), (gk, gk_hbm), (ghq, ghq_hbm), (ghk, ghk_hbm),
                (ghv, ghv_hbm),
            ]
        )
    ]

    barrier = pltpu.get_barrier_semaphore()
    for d in range(1, count):
        pl.semaphore_signal(barrier, inc=1, device_id=token(me + d), device_id_type=MESH)
    for d in range(1, tensors):
        pl.semaphore_signal(barrier, inc=1, device_id=peer(ten + d), device_id_type=MESH)
    pl.semaphore_wait(barrier, count - 1 + tensors - 1)

    def copy(slot, src, dst, device):
        return pltpu.make_async_remote_copy(
            src_ref=src, dst_ref=dst, send_sem=send.at[slot], recv_sem=recv.at[slot],
            device_id=device, device_id_type=MESH,
        )

    first, last = ctx == 0, ctx == contexts - 1
    inner_lo, inner_hi = jnp.logical_not(first), jnp.logical_not(last)
    core0, core1 = mir == 0, mir == 1
    partner = token(me + 1 - 2 * mir)

    span = channels // CHUNKS
    own_tail = pl.ds(rows, taps)
    has_lo, has_hi = me > 0, me < count - 1

    def cut(c):
        return pl.ds(c * span, span)

    def chunked(slot, src, src_rows, dst, dst_rows, device):
        return [
            copy(slot * CHUNKS + c, src.at[src_rows, cut(c)], dst.at[dst_rows, cut(c)], device)
            for c in range(CHUNKS)
        ]

    c_kv = chunked(KV, kvwin, own_tail, kvwin, pl.ds(0, taps), token(me + 1))
    c_gs = chunked(GS, gswin, pl.ds(0, taps), gswin, pl.ds(rows, taps), token(me - 1))

    def forward(slot2, slot1, win):
        return (
            chunked(slot2, win, near, win, far, token(me + 2)),
            chunked(slot1, win, near, win, mid, partner),
            chunked(slot1, win, far, win, mid, partner),
        )

    def backward(slot2, slot1, win):
        return (
            chunked(slot2, win, far, win, near, token(me - 2)),
            chunked(slot1, win, far, win, mid, partner),
            chunked(slot1, win, near, win, mid, partner),
        )

    k_cp = forward(K2, K1, kwin)
    v_cp = forward(V2, V1, vwin)
    q_cp = backward(Q2, Q1, qwin)
    d_cp = backward(D2, D1, dwin)
    few = heads // CHUNKS

    def rows_back(slot1, slot2, ref):
        def one(slot, to, c, device):
            at = pl.ds(c * few, few)
            return copy(slot * CHUNKS + c, ref.at[0, at], ref.at[to, at], device)

        return (
            [one(slot1, 1, c, token(me - 1)) for c in range(CHUNKS)],
            [one(slot2, 2, c, token(me - 2)) for c in range(CHUNKS)],
        )

    l_cp = rows_back(L1, L2, lrow)
    e_cp = rows_back(E1, E2, erow)

    def when(cond, fn):
        pl.when(cond)(fn)

    def start_forward(cps, c):
        when(inner_hi, cps[0][c].start)
        when(core0, cps[1][c].start)

    def start_backward(cps, c):
        when(inner_lo, cps[0][c].start)
        when(core1, cps[1][c].start)

    def land_forward(cps, c):
        when(inner_lo, cps[0][c].wait_recv)
        when(jnp.logical_and(core1, inner_lo), cps[2][c].start)

    def land_backward(cps, c):
        when(inner_hi, cps[0][c].wait_recv)
        when(jnp.logical_and(core0, inner_hi), cps[2][c].start)

    def finish_forward(cps, c):
        when(jnp.logical_or(core1, inner_lo), cps[1][c].wait_recv)

    def finish_backward(cps, c):
        when(jnp.logical_or(core0, inner_hi), cps[1][c].wait_recv)

    def start_rows(cps, c):
        when(me > 0, cps[0][c].start)
        when(me > 1, cps[1][c].start)

    def finish_rows(cps, c):
        when(me < count - 1, cps[0][c].wait_recv)
        when(me < count - 2, cps[1][c].wait_recv)

    def drain_forward(cps, c):
        when(inner_hi, cps[0][c].wait_send)
        when(core0, cps[1][c].wait_send)
        when(jnp.logical_and(core1, inner_lo), cps[2][c].wait_send)

    def drain_backward(cps, c):
        when(inner_lo, cps[0][c].wait_send)
        when(core1, cps[1][c].wait_send)
        when(jnp.logical_and(core0, inner_hi), cps[2][c].wait_send)

    loads[0].wait()
    start_backward(q_cp, 0)
    loads[1].wait()
    loads[2].wait()
    kvwin[pl.ds(taps, rows)] = (hk[...].astype(F32) * hv[...].astype(F32)).astype(BF16)
    for c in range(CHUNKS):
        when(has_hi, c_kv[c].start)
    loads[3].wait()
    start_forward(k_cp, 0)
    loads[4].wait()
    start_backward(d_cp, 0)
    start_backward(q_cp, 1)
    start_forward(k_cp, 1)

    def zero(ref, at):
        ref[at] = jnp.zeros((ref[at].shape), ref.dtype)

    when(me == 0, lambda: zero(kvwin, pl.ds(0, taps)))
    when(me == count - 1, lambda: zero(gswin, pl.ds(rows, taps)))
    when(first, lambda: zero(kwin, far))
    when(first, lambda: zero(vwin, far))
    when(me == 0, lambda: zero(kwin, mid))
    when(me == 0, lambda: zero(vwin, mid))
    when(last, lambda: zero(qwin, near))
    when(last, lambda: zero(dwin, near))
    when(me == count - 1, lambda: zero(qwin, mid))
    when(me == count - 1, lambda: zero(dwin, mid))
    when(me == count - 1, lambda: zero(lrow, 1))
    when(me == count - 1, lambda: zero(erow, 1))
    when(me >= count - 2, lambda: zero(lrow, 2))
    when(me >= count - 2, lambda: zero(erow, 2))

    row_at = lax.broadcasted_iota(jnp.int32, (taps, taps), 0)
    col_at = lax.broadcasted_iota(jnp.int32, (taps, taps), 1)
    turn = jnp.where(lax.rem(row_at + col_at, taps) == 0, 1.0, 0.0).astype(BF16)
    filt[...] = filt_in[...].astype(F32)
    filt_rev[...] = dot_nn(filt_in[...], turn)

    ends = []
    total = jnp.int32(0)
    for i in range(lens.shape[0]):
        total = total + lens[i]
        ends.append(total)

    def doc(pos):
        return sum((pos >= e).astype(jnp.int32) for e in ends)

    def grid(shape, row0, col0):
        return (
            row0 + lax.broadcasted_iota(jnp.int32, shape, 0),
            col0 + lax.broadcasted_iota(jnp.int32, shape, 1),
        )

    t_pos, u_pos = grid((rows, 3 * rows), base, base - 2 * rows)
    ok = (u_pos >= 0) & (u_pos <= t_pos) & (t_pos - u_pos <= REACH * rows) & (doc(u_pos) == doc(t_pos))
    qbias[...] = jnp.where(ok, 0.0, NEG)
    u_pos, t_pos = grid((rows, 3 * rows), base, base)
    ok = (u_pos <= t_pos) & (t_pos - u_pos <= REACH * rows) & (doc(u_pos) == doc(t_pos))
    kbias[...] = jnp.where(ok, 0.0, NEG)
    for s in range(subs):
        at = pl.ds(s * taps, taps)
        t_pos, u_pos = grid((taps, 2 * taps), base + s * taps, base + (s - 1) * taps)
        ok = (u_pos >= 0) & (u_pos <= t_pos) & (t_pos - u_pos < taps) & (doc(u_pos) == doc(t_pos))
        fmask[at] = jnp.where(ok, 1.0, 0.0).astype(BF16)
        halves = []
        for i in range(2):
            t_pos, w_pos = grid((taps, taps), base + s * taps, 0)
            u_pos = base + (s - 1 + i) * taps + lax.rem(taps - w_pos, taps)
            ok = (u_pos >= 0) & (u_pos <= t_pos) & (t_pos - u_pos < taps) & (doc(u_pos) == doc(t_pos))
            halves.append(jnp.where(ok, 1.0, 0.0))
        rmask[at] = jnp.concatenate(halves, axis=1)
        t_pos, u_pos = grid((taps, 2 * taps), base + s * taps, base + s * taps)
        ok = (u_pos >= t_pos) & (u_pos - t_pos < taps) & (doc(u_pos) == doc(t_pos))
        bmask[at] = jnp.where(ok, 1.0, 0.0).astype(BF16)

    lane = lax.broadcasted_iota(jnp.int32, (taps, LANES), 1)

    def chan(b):
        return pl.ds(pl.multiple_of(b * LANES, LANES), LANES)

    def toeplitz(ref, b):
        made = []
        for i in range(per):
            row = jnp.broadcast_to(ref[pl.ds(b * per + i, 1), :], (taps, taps))
            made.append(pltpu.roll(row, 0, 1, stride=1, stride_axis=0).astype(BF16))
        return made

    def stacked(bands, mask):
        mask_lo, mask_hi = mask[:, :taps], mask[:, taps:]
        return jnp.concatenate(
            [jnp.concatenate([band * mask_lo, band * mask_hi], axis=1) for band in bands], axis=0
        )

    def conv(stack, window):
        every = dot_nn(stack, window)
        picked = every[:taps]
        for i in range(1, per):
            picked = jnp.where(lane >= i * width, every[i * taps : (i + 1) * taps], picked)
        return picked

    early = bands_back.shape[0] == blocks

    def band_step(b, carry):
        bands_back[b] = stacked(toeplitz(filt, b), bmask[...])
        return carry

    if early:
        lax.fori_loop(0, blocks, band_step, 0, unroll=2)

    start_backward(d_cp, 1)
    loads[5].wait()

    def signal_step(b, acc):
        at = chan(b)
        bands = toeplitz(filt_rev, b)
        parts = []
        for s in range(subs):
            here = pl.ds(s * taps, taps)
            made = conv(stacked(bands, fmask[here]), kvwin[pl.ds(s * taps, 2 * taps), at])
            signal[here, at] = made
            mix = hq[here, at].astype(F32) * made
            parts.append(mix * mix)
        for s in range(subs + 1):
            here = pl.ds(s * taps, taps)
            kvturn[here, at] = dot_nn(turn, kvwin[here, at]).astype(BF16)
        return acc + jnp.concatenate(parts, axis=0)

    col_lane = lax.broadcasted_iota(jnp.int32, (rows, LANES), 1)

    def lse_step(h, acc):
        at = chan(h)
        score = dot_nt(qwin[far, at], kwin[:, at]) * scale + qbias[...]
        top = jnp.max(score, axis=1, keepdims=True)
        raised = jnp.exp(score - top)
        total = jnp.sum(raised, axis=1, keepdims=True)
        lse = top + jnp.log(total)
        prob[h] = raised * (1.0 / total)
        return jnp.where(col_lane == h, lse, acc)

    zeros = jnp.zeros((rows, LANES), F32)

    def over_heads(step, c, acc, unroll=4):
        return lax.fori_loop(c * few, (c + 1) * few, step, acc, unroll=unroll)

    def wide_row(ref, h):
        return jnp.concatenate([ref[j, pl.ds(h, 1), :] for j in range(3)], axis=1)

    def gval_step(h, acc):
        at = chan(h)
        score = dot_nt(kwin[near, at], qwin[:, at]) * scale + kbias[...]
        p = jnp.exp(score - wide_row(lrow, h))
        prob_t[h] = p
        made = dot_nn(p.astype(BF16), dwin[:, at])
        gval[:, at] = made
        return acc + gain[:, at] * made * (hq[:, at].astype(F32) * signal[:, at])

    def exchange(which, partial):
        total = jnp.sum(partial, axis=1, keepdims=True)
        cols[...] = jnp.where(col_lane == 0, total, 0.0)
        stat_out[which] = jnp.transpose(cols[...])[:8]
        cps = [
            copy(
                FIXED + which * (tensors - 1) + d - 1,
                stat_out.at[which], stat_in.at[which, d - 1], peer(ten + d),
            )
            for d in range(1, tensors)
        ]
        for c in cps:
            c.start()
        return cps

    def exchanged(which, cps):
        for c in cps:
            c.wait_recv()
        stats = stat_out[which]
        for d in range(1, tensors):
            stats = stats + stat_in[which, d - 1]
        stats = jnp.concatenate([stats, jnp.zeros((LANES - 8, rows), F32)], axis=0)
        return jnp.transpose(stats)[:, 0:1]

    def lse_chunk(c):
        finish_forward(k_cp, c)
        cols[...] = over_heads(lse_step, c, zeros)
        lrow[0, c * few : (c + 1) * few] = jnp.transpose(cols[...])[c * few : (c + 1) * few]
        start_rows(l_cp, c)

    squares = inner = zeros
    for c in range(CHUNKS):
        when(has_lo, c_kv[c].wait_recv)
        squares = over_heads(signal_step, c, squares, 2)
        if c == 0:
            land_forward(k_cp, 0)
    square_cp = exchange(0, squares)
    lse_chunk(0)
    land_forward(k_cp, 1)
    inv = lax.rsqrt(exchanged(0, square_cp) / D + 1e-06)

    def value_step(b, carry):
        at = chan(b)
        mix = hq[:, at].astype(F32) * signal[:, at]
        vwin[near, at] = (mix * inv * gain[:, at]).astype(BF16)
        return carry

    for c in range(CHUNKS):
        over_heads(value_step, c, 0)
        start_forward(v_cp, c)
    land_backward(q_cp, 0)
    land_backward(d_cp, 0)
    lse_chunk(1)

    land_backward(q_cp, 1)
    finish_backward(q_cp, 0)
    finish_backward(d_cp, 0)
    finish_rows(l_cp, 0)
    inner = over_heads(gval_step, 0, inner)
    land_backward(d_cp, 1)
    land_forward(v_cp, 0)
    finish_backward(q_cp, 1)
    finish_backward(d_cp, 1)
    finish_rows(l_cp, 1)
    inner = over_heads(gval_step, 1, inner)
    inner_cp = exchange(1, inner)
    land_forward(v_cp, 1)

    def query_step(h, acc):
        at = chan(h)
        values = vwin[:, at]
        p = prob[h]
        grad_p = dot_nt(dwin[far, at], values)
        out[:, at] = dot_nn(p.astype(BF16), values).astype(BF16)
        delta = jnp.sum(p * grad_p, axis=1, keepdims=True)
        ds = (p * (grad_p - delta) * scale).astype(BF16)
        gq[:, at] = dot_nn(ds, kwin[:, at]).astype(BF16)
        return jnp.where(col_lane == h, delta, acc)

    def query_chunk(c):
        finish_forward(v_cp, c)
        cols[...] = over_heads(query_step, c, zeros)
        erow[0, c * few : (c + 1) * few] = jnp.transpose(cols[...])[c * few : (c + 1) * few]
        start_rows(e_cp, c)
    query_chunk(0)
    pull = exchanged(1, inner_cp) * inv * inv / D

    def norm_step(b, carry):
        at = chan(b)
        gate = hq[:, at].astype(F32)
        made = signal[:, at]
        grad_mix = inv * (gain[:, at] * gval[:, at] - gate * made * pull)
        ghq[:, at] = (grad_mix * made).astype(BF16)
        gswin[pl.ds(0, rows), at] = (grad_mix * gate).astype(BF16)
        return carry

    for c in range(CHUNKS):
        over_heads(norm_step, c, 0)
        when(has_lo, c_gs[c].start)
    stores[3].start()
    for c in range(1, CHUNKS):
        query_chunk(c)
    stores[0].start()
    stores[1].start()

    def filter_step(b, carry):
        at = chan(b)
        sums = [jnp.zeros((1, taps), F32) for _ in range(per)]
        for s in range(subs):
            grads = gswin[pl.ds(s * taps, taps), at]
            stack = jnp.concatenate(
                [
                    jnp.where((lane >= i * width) & (lane < (i + 1) * width), grads, jnp.zeros_like(grads))
                    for i in range(per)
                ],
                axis=0,
            )
            every = dot_nt(stack, kvturn[pl.ds(s * taps, 2 * taps), at])
            mask = rmask[pl.ds(s * taps, taps)]
            for i in range(per):
                part = every[i * taps : (i + 1) * taps] * mask
                part = part[:, :taps] + part[:, taps:]
                part = pltpu.roll(part, 0, 1, stride=1, stride_axis=0)
                sums[i] = sums[i] + jnp.sum(part, axis=0, keepdims=True)
        gflat[pl.ds(pl.multiple_of(b * per, per), per), :] = jnp.concatenate(sums, axis=0)
        return carry

    lax.fori_loop(0, blocks, filter_step, 0, unroll=2)
    share = groups // count
    for i in range(count):
        gpart[i] = gflat[i * share : (i + 1) * share]
    at0 = FIXED + 2 * (tensors - 1)
    scatter = [
        copy(at0 + d - 1, gpart.at[lax.rem(me + d, count)], gin.at[d - 1], token(me + d))
        for d in range(1, count)
    ]
    for c in scatter:
        c.start()

    def back_step(b, carry):
        at = chan(b)
        bands = None if early else toeplitz(filt, b)
        for s in range(subs):
            here = pl.ds(s * taps, taps)
            stack = bands_back[b] if early else stacked(bands, bmask[here])
            made = conv(stack, gswin[pl.ds(s * taps, 2 * taps), at])
            ghk[here, at] = (made * hv[here, at].astype(F32)).astype(BF16)
            ghv[here, at] = (made * hk[here, at].astype(F32)).astype(BF16)
        return carry

    at1 = at0 + count - 1
    gather = [
        copy(at1 + d - 1, gsum.at[me], gsum.at[me], token(me + d)) for d in range(1, count)
    ]

    for c in range(CHUNKS):
        when(has_hi, c_gs[c].wait_recv)
    lax.fori_loop(0, blocks, back_step, 0, unroll=2)
    stores[4].start()
    stores[5].start()
    for d in scatter:
        d.wait_recv()
    mine = gpart[me]
    for d in range(1, count):
        mine = mine + gin[d - 1]
    gsum[me] = mine
    for d in gather:
        d.start()

    def key_step(h, carry):
        at = chan(h)
        grad_p = dot_nt(vwin[near, at], dwin[:, at])
        ds = (prob_t[h] * (grad_p - wide_row(erow, h)) * scale).astype(BF16)
        gk[:, at] = dot_nn(ds, qwin[:, at]).astype(BF16)
        return carry

    for c in range(CHUNKS):
        finish_rows(e_cp, c)
    lax.fori_loop(0, heads, key_step, 0, unroll=4)
    stores[2].start()

    for d in range(1, count):
        other = lax.rem(me - d + count, count)
        copy(at1 + d - 1, gsum.at[other], gsum.at[other], token(me + d)).wait_recv()
    for i in range(count):
        gfilt[i * share : (i + 1) * share] = gsum[i]

    for c in range(CHUNKS):
        when(has_hi, c_kv[c].wait_send)
        when(has_lo, c_gs[c].wait_send)
        drain_forward(k_cp, c)
        drain_forward(v_cp, c)
        drain_backward(q_cp, c)
        drain_backward(d_cp, c)
        for cps in (l_cp, e_cp):
            when(me > 0, cps[0][c].wait_send)
            when(me > 1, cps[1][c].wait_send)
    for c in square_cp + inner_cp + scatter + gather:
        c.wait_send()
    for c in stores:
        c.wait()


def hand_on(*refs):
    count = (len(refs) - 2) // 3
    sources, results, held = refs[:count], refs[count : 2 * count], refs[2 * count : 3 * count]
    came, went = refs[-2:]
    loads = [pltpu.make_async_copy(sources[i], held[i], came.at[i]) for i in range(count)]
    stores = [pltpu.make_async_copy(held[i], results[i], went.at[i]) for i in range(count)]
    for c in loads:
        c.start()
    for first, then in zip(loads, stores):
        first.wait()
        then.start()
    for c in stores:
        c.wait()


def body(dims, hyena_q, hyena_k, hyena_v, filters, norm_gain, attn_q, attn_k, out_grad, doc_lengths):
    contexts, mirrors, tensors = dims
    count = contexts * mirrors
    rows, channels = hyena_q.shape
    groups, taps = filters.shape
    heads = channels // HEAD
    share = groups // count
    slots = FIXED + 2 * (tensors - 1) + 2 * (count - 1)
    window = (3 * rows, channels)
    tile = jax.ShapeDtypeStruct((rows, channels), BF16)
    vmem = pl.BlockSpec(memory_space=pltpu.VMEM)
    hbm = pl.BlockSpec(memory_space=pl.ANY)
    blocks = channels // LANES
    band_shape = (blocks, groups // blocks * taps, 2 * taps) if rows == taps else (1, 8, LANES)
    results = pl.pallas_call(
        functools.partial(kernel, dims),
        out_shape=(tile,) * 6 + (jax.ShapeDtypeStruct((groups, taps), F32),),
        in_specs=[hbm] * 3 + [vmem] * 2 + [hbm] * 3 + [pl.BlockSpec(memory_space=pltpu.SMEM)],
        out_specs=(hbm,) * 6 + (vmem,),
        scratch_shapes=[pltpu.VMEM((rows, channels), BF16)] * 9
        + [
            pltpu.VMEM(band_shape, BF16),
            pltpu.VMEM((groups, taps), F32),
            pltpu.VMEM((groups, taps), F32),
            pltpu.VMEM((taps + rows, channels), BF16),
            pltpu.VMEM((taps + rows, channels), BF16),
            pltpu.VMEM((taps + rows, channels), BF16),
            pltpu.VMEM(window, BF16),
            pltpu.VMEM(window, BF16),
            pltpu.VMEM(window, BF16),
            pltpu.VMEM(window, BF16),
            pltpu.VMEM((3, heads, rows), F32),
            pltpu.VMEM((3, heads, rows), F32),
            pltpu.VMEM((heads, rows, 3 * rows), F32),
            pltpu.VMEM((heads, rows, 3 * rows), F32),
            pltpu.VMEM((rows, 3 * rows), F32),
            pltpu.VMEM((rows, 3 * rows), F32),
            pltpu.VMEM((rows, 2 * taps), BF16),
            pltpu.VMEM((rows, 2 * taps), BF16),
            pltpu.VMEM((rows, 2 * taps), F32),
            pltpu.VMEM((rows, channels), F32),
            pltpu.VMEM((rows, channels), F32),
            pltpu.VMEM((rows, LANES), F32),
            pltpu.VMEM((2, 8, rows), F32),
            pltpu.VMEM((2, tensors - 1, 8, rows), F32),
            pltpu.VMEM((groups, taps), F32),
            pltpu.VMEM((count, share, taps), F32),
            pltpu.VMEM((count - 1, share, taps), F32),
            pltpu.VMEM((count, share, taps), F32),
            pltpu.SemaphoreType.DMA((slots,)),
            pltpu.SemaphoreType.DMA((slots,)),
            pltpu.SemaphoreType.DMA((6,)),
            pltpu.SemaphoreType.DMA((6,)),
        ],
        compiler_params=pltpu.CompilerParams(
            collective_id=0, has_side_effects=True, vmem_limit_bytes=VMEM_MOST
        ),
        name="hyena_attention",
    )(
        hyena_q, hyena_k, hyena_v, filters, norm_gain[None, :], attn_q, attn_k, out_grad,
        doc_lengths,
    )
    shapes = [jax.ShapeDtypeStruct(r.shape, r.dtype) for r in results]
    return pl.pallas_call(
        hand_on,
        out_shape=tuple(shapes),
        in_specs=[hbm] * len(shapes),
        out_specs=(hbm,) * len(shapes),
        scratch_shapes=[pltpu.VMEM(x.shape, x.dtype) for x in shapes]
        + [pltpu.SemaphoreType.DMA((len(shapes),))] * 2,
        compiler_params=pltpu.CompilerParams(vmem_limit_bytes=VMEM_MOST),
        name="hand_on",
    )(*results)


def solution(mesh):
    dims = (mesh.shape["context"], mesh.shape["mirror"], mesh.shape["tensor"])
    tokens = P(("context", "mirror"), "tensor")
    return jax.shard_map(
        functools.partial(body, dims),
        mesh=mesh,
        in_specs=(tokens, tokens, tokens, P("tensor", None), P("tensor"), tokens, tokens, tokens, P()),
        out_specs=(tokens,) * 6 + (P("tensor", None),),
        check_vma=False,
    )
```
